128 devices in a mesh: lat: 8 (over x, core), lon: 16 (over z, y).
Axes of the slice: x: 4, y: 4, z: 4, core: 2. Of those that a mesh axis runs over, the one named last changes fastest.
Arguments:
- spectrum: float32 [640, 640, 512], P(('lat', 'lon')), may hold values from -6 to 6
- legendre: float32 [640, 320, 640], P(('lat', 'lon')), may hold values from -0.25 to 0.25
- wave_table: int32 [640], replicated, may hold values from 0 to 639, each once
- quad_weight: float32 [320], replicated, may hold values from 10 to 40
- norm_gain: float32 [256], replicated, may hold values from 0.5 to 1.5
- weight_in: float32 [256, 512], replicated, may hold values from -0.375 to 0.375
- bias_in: float32 [512], replicated, may hold values from -3 to 3
- weight_out: float32 [512, 256], replicated, may hold values from -0.25 to 0.25
Outputs:
- spectrum_tend: float32 [640, 640, 512], P(('lat', 'lon'))
The draws below stay inside these ranges and needn't reach their ends.
Inputs may be any that keep to these rules, and one draw needn't show every extreme that they name: `wave_table`: entry s is the zonal wavenumber of slot s of the spectral arrays and of legendre; each of 0 to 639 appears once.
All inputs are finite; a program needn't handle non-finite values.
Results may differ from the reference program's by a relative error of at most 0.0003.
Values sent between devices are 32-bit elements; how exact they have to be, the bound alone decides.
No kernel may reach another device: no remote copies, remote signals or barrier semaphores. Data moves between devices by JAX's collectives and lax.ppermute only.
A program may use at most 128 MiB of HBM per device.

```python
import math
import jax
import jax.numpy as jnp
from jax import lax

M = 640
HIDDEN_SIZE = 512
C = 256
HALF = 320
NLON = 1280


def steps_of(rng, dims, shards, least, largest):
    level = 1.0
    for axis_at, shards_of in shards:
        heights = jax.random.uniform(jax.random.fold_in(jax.random.fold_in(rng, 6), axis_at), (shards_of,), jnp.float32, least / len(shards), largest / len(shards))
        level = level * jnp.repeat(jnp.exp(heights), dims[axis_at] // shards_of).reshape((-1,) + (1,) * (len(dims) - 1 - axis_at))
    return level


def normal_values(stream_key, extent, deviation, bound, pieces=(), held_as=jnp.bfloat16):
    gain = steps_of(stream_key, extent, pieces, -0.22, 0.18) if pieces else 1.0
    drawn = jax.random.normal(stream_key, extent, jnp.float32) * deviation * gain
    return jnp.minimum(jnp.maximum(drawn, -bound), bound).astype(held_as)


def setup_inputs(seed: int = 0) -> dict:
    streams_of = jax.random.split(jax.random.key(seed), 9)
    return {
        "spectrum": normal_values(streams_of[0], (M, M, 2 * C), 1.0, 6.0, ((0, 128),), jnp.float32),
        "legendre": normal_values(streams_of[1], (M, HALF, M), M ** -0.5, 0.25, ((0, 128),), jnp.float32),
        "wave_table": jax.random.permutation(streams_of[2], M).astype(jnp.int32),
        "quad_weight": jnp.clip(jnp.exp(jax.random.uniform(streams_of[3], (HALF,), jnp.float32, math.log(10.0), math.log(40.0))), 10.0, 40.0),
        "norm_gain": jnp.clip(jax.random.uniform(streams_of[4], (C,), jnp.float32, 0.5, 1.5), 0.5, 1.5),
        "weight_in": normal_values(streams_of[5], (C, HIDDEN_SIZE), C ** -0.5, 0.375, (), jnp.float32),
        "bias_in": normal_values(streams_of[6], (HIDDEN_SIZE,), 0.5, 3.0, (), jnp.float32),
        "weight_out": normal_values(streams_of[7], (HIDDEN_SIZE, C), HIDDEN_SIZE ** -0.5, 0.25, (), jnp.float32),
    }


def reference(spectrum, legendre, wave_table, quad_weight, norm_gain, weight_in, bias_in, weight_out):
    degrees = jnp.arange(M, dtype=jnp.int32)

    def synth_slot(packed):
        table_row, coeffs, wave_number = packed
        kept_mask = (degrees >= wave_number).astype(jnp.float32)
        imag_keep = jnp.where(wave_number > 0, 1.0, 0.0).astype(jnp.float32)
        part_scale = jnp.concatenate([jnp.ones((C,), jnp.float32), jnp.ones((C,), jnp.float32) * imag_keep])
        masked = coeffs * kept_mask[:, None] * part_scale[None, :]
        parity_sign = jnp.where((degrees + wave_number) % 2 == 0, 1.0, -1.0).astype(jnp.float32)
        northern = jnp.dot(table_row, masked, precision=lax.Precision.HIGHEST, preferred_element_type=jnp.float32)
        southern = jnp.dot(table_row * parity_sign[None, :], masked, precision=lax.Precision.HIGHEST, preferred_element_type=jnp.float32)
        return jnp.concatenate([northern, southern], axis=0)
    fourier = lax.map(synth_slot, (legendre, spectrum, wave_table))
    fourier_modes = fourier[..., :C] + 1j * fourier[..., C:]
    spectrum_full = jnp.zeros((M + 1, M, C), fourier_modes.dtype).at[wave_table].set(fourier_modes)
    by_rows = jnp.transpose(spectrum_full, (1, 0, 2)).reshape(M // 8, 8, M + 1, C)

    def physics_block(row_block):
        columns = jnp.fft.irfft(row_block, n=NLON, axis=1) * NLON
        mean_square = lax.optimization_barrier(jnp.mean(columns * columns, axis=-1, keepdims=True))
        normed = columns * norm_gain / jnp.sqrt(mean_square + 1e-06)
        flat_columns = normed.reshape(-1, C)
        hidden = jax.nn.silu(jnp.dot(flat_columns, weight_in, precision=lax.Precision.HIGHEST, preferred_element_type=jnp.float32) + bias_in)
        tendency = jnp.dot(hidden, weight_out, precision=lax.Precision.HIGHEST, preferred_element_type=jnp.float32).reshape(columns.shape)
        modes_back = jnp.fft.rfft(tendency, axis=1) / NLON
        picked = modes_back[:, wave_table, :]
        return jnp.concatenate([jnp.real(picked), jnp.imag(picked)], axis=-1).astype(jnp.float32)
    returned = lax.map(physics_block, by_rows).reshape(M, M, 2 * C)
    returned = jnp.transpose(returned, (1, 0, 2))

    def analyse_slot(packed):
        table_row, wave_number, rows_back = packed
        kept_mask = (degrees >= wave_number).astype(jnp.float32)
        parity_sign = jnp.where((degrees + wave_number) % 2 == 0, 1.0, -1.0).astype(jnp.float32)
        weighted = table_row * quad_weight[:, None]
        northern = rows_back[:HALF]
        southern = rows_back[HALF:]
        projected = jnp.dot(weighted.T, northern, precision=lax.Precision.HIGHEST, preferred_element_type=jnp.float32)
        projected = projected + jnp.dot((weighted * parity_sign[None, :]).T, southern, precision=lax.Precision.HIGHEST, preferred_element_type=jnp.float32)
        return projected * kept_mask[:, None]
    return lax.map(analyse_slot, (legendre, wave_table, returned))
```

```python
import functools
import math

import jax
import jax.numpy as jnp
from jax import lax
from jax.experimental import pallas as pl
from jax.experimental.pallas import tpu as pltpu
from jax.sharding import PartitionSpec as P

M = 640
C = 256
HALF = 320
NLON = 1280
HIDDEN = 512
DEVICES = 128
SLOTS = M // DEVICES
LANES = 128
QB = 2 * C // LANES
BLOCK = 64
KPAD = 672
KBLOCKS = 3
KB = KPAD // KBLOCKS
AXES = ("lat", "lon")
VMEM_LIMIT = 56 * 1024 * 1024
F32 = jnp.float32
BF16 = jnp.bfloat16

CHUNKS = (
    (((0, False), (1, False)), ((0, True), (1, True))),
    (((2, False), (3, False)), ((2, True), (3, True)), ((4, False), (4, True))),
)


def blocks_of(chunk):
    return sorted({block for row in chunk for block, _ in row})


def split(value):
    high = value.astype(BF16)
    low = (value - high.astype(F32)).astype(BF16)
    return high, low


def dot3(left, right):
    dot = functools.partial(jnp.dot, preferred_element_type=F32)
    return dot(left[0], right[0]) + (dot(left[0], right[1]) + dot(left[1], right[0]))


def synth_kernel(chunk, waves_ref, spec_ref, *refs):
    blocks = blocks_of(chunk)
    leg_refs, out_ref = refs[: len(blocks)], refs[len(blocks)]
    rows = len(chunk)
    slot = pl.program_id(0)
    wave = waves_ref[slot]
    degrees = lax.broadcasted_iota(jnp.int32, (M, 1), 0)
    imag_keep = jnp.where(wave > 0, 1.0, 0.0).astype(F32)
    lanes = lax.broadcasted_iota(jnp.int32, (1, 2 * C), 1)
    scale = jnp.where(lanes < C, 1.0, imag_keep)
    coef = split(jnp.where(degrees >= wave, spec_ref[0] * scale, 0.0))
    across = lax.broadcasted_iota(jnp.int32, (1, M), 1)
    sign = jnp.where((across + wave) % 2 == 0, 1.0, -1.0).astype(F32)
    tables = {}
    for block, ref in zip(blocks, leg_refs):
        tables[block, False] = ref[0]
        tables[block, True] = ref[0] * sign
    for i, row in enumerate(chunk):
        table = jnp.concatenate([tables[piece] for piece in row], axis=0)
        fourier = dot3(split(table), coef)
        for b in range(QB):
            out_ref[pl.ds((slot * rows + i) * QB + b, DEVICES, stride=SLOTS * rows * QB), :] = (
                fourier[:, b * LANES : (b + 1) * LANES]
            )


def synth(chunk, own_waves, spectrum, legendre):
    blocks = blocks_of(chunk)
    rows = len(chunk)
    total = M * rows * QB
    return pl.pallas_call(
        functools.partial(synth_kernel, chunk),
        out_shape=jax.ShapeDtypeStruct((total, LANES), F32),
        grid=(SLOTS,),
        in_specs=[
            pl.BlockSpec(memory_space=pltpu.SMEM),
            pl.BlockSpec((1, M, 2 * C), lambda s: (s, 0, 0)),
        ]
        + [pl.BlockSpec((1, BLOCK, M), lambda s, k=k: (s, k, 0)) for k in blocks],
        out_specs=pl.BlockSpec((total, LANES), lambda s: (0, 0)),
        compiler_params=pltpu.CompilerParams(vmem_limit_bytes=VMEM_LIMIT),
        cost_estimate=pl.CostEstimate(
            flops=6 * SLOTS * DEVICES * rows * M * 2 * C,
            bytes_accessed=4 * (SLOTS * M * 2 * C * 2 + total * LANES),
            transcendentals=0,
        ),
        name="legendre_synthesis",
    )(own_waves, spectrum, *([legendre] * len(blocks)))


def physics_kernel(
    rows,
    x_ref,
    cos_ref,
    sin_ref,
    cost_ref,
    sint_ref,
    gain_ref,
    win_ref,
    bias_ref,
    wout_ref,
    out_ref,
    syn_ref,
    ana_ref,
    w1_ref,
    w2_ref,
    tend_ref,
):
    row = pl.program_id(0)

    @pl.when(row == 0)
    def _():
        for j, ref in enumerate((cos_ref, sin_ref)):
            syn_ref[2 * j], syn_ref[2 * j + 1] = split(ref[...])
        for j, ref in enumerate((cost_ref, sint_ref)):
            ana_ref[2 * j], ana_ref[2 * j + 1] = split(ref[...])
        w1_ref[0], w1_ref[1] = split(win_ref[...])
        w2_ref[0], w2_ref[1] = split(wout_ref[...])

    step = rows * QB
    parts = [x_ref[pl.ds(row * QB + b, M, stride=step), :] for b in range(QB)]
    real = split(jnp.concatenate(parts[: QB // 2], axis=1))
    imag = split(jnp.concatenate(parts[QB // 2 :], axis=1))
    w1 = (w1_ref[0], w1_ref[1])
    w2 = (w2_ref[0], w2_ref[1])
    for k in range(KBLOCKS):
        rng = slice(k * KB, (k + 1) * KB)
        even = dot3((syn_ref[0, rng, :], syn_ref[1, rng, :]), real)
        odd = dot3((syn_ref[2, rng, :], syn_ref[3, rng, :]), imag)
        columns = jnp.concatenate([even - odd, even + odd], axis=0)
        mean_square = jnp.mean(columns * columns, axis=-1, keepdims=True)
        normed = columns * gain_ref[...] * lax.rsqrt(mean_square + 1e-06)
        hidden = dot3(split(normed), w1) + bias_ref[...]
        hidden = hidden / (1.0 + jnp.exp(-hidden))
        tendency = dot3(split(hidden), w2)
        plus, minus = tendency[:KB], tendency[KB:]
        tend_ref[0, rng, :], tend_ref[1, rng, :] = split(plus + minus)
        tend_ref[2, rng, :], tend_ref[3, rng, :] = split(plus - minus)
    back = [
        dot3((ana_ref[j], ana_ref[j + 1]), (tend_ref[j], tend_ref[j + 1])) for j in (0, 2)
    ]
    for b in range(QB):
        part = back[b // 2][:, (b % 2) * LANES : (b % 2 + 1) * LANES]
        out_ref[pl.ds(row * QB + b, M, stride=step), :] = part


def physics(rows, arrived, tables, gain, weight_in, bias, weight_out):
    total = M * rows * QB
    whole = lambda shape: pl.BlockSpec(shape, lambda r: (0,) * len(shape))
    operands = (arrived, *tables, gain, weight_in, bias, weight_out)
    return pl.pallas_call(
        functools.partial(physics_kernel, rows),
        out_shape=jax.ShapeDtypeStruct((total, LANES), F32),
        grid=(rows,),
        in_specs=[whole(x.shape) for x in operands],
        out_specs=whole((total, LANES)),
        scratch_shapes=[
            pltpu.VMEM((4, KPAD, M), BF16),
            pltpu.VMEM((4, M, KPAD), BF16),
            pltpu.VMEM((2, C, HIDDEN), BF16),
            pltpu.VMEM((2, HIDDEN, C), BF16),
            pltpu.VMEM((4, KPAD, C), BF16),
        ],
        compiler_params=pltpu.CompilerParams(vmem_limit_bytes=VMEM_LIMIT),
        cost_estimate=pl.CostEstimate(
            flops=6 * rows * KPAD * (4 * M * C + 4 * C * HIDDEN),
            bytes_accessed=8 * total * LANES + 16 * KPAD * M,
            transcendentals=2 * rows * KPAD * HIDDEN,
        ),
        name="column_physics",
    )(*operands)


def analyse_kernel(chunk, partial, waves_ref, arrived_ref, weight_ref, *refs):
    blocks = blocks_of(chunk)
    leg_refs = refs[: len(blocks)]
    out_ref = refs[-1]
    rows = len(chunk)
    slot = pl.program_id(0)
    wave = waves_ref[slot]
    degrees = lax.broadcasted_iota(jnp.int32, (M, 1), 0)
    sign = jnp.where((degrees + wave) % 2 == 0, 1.0, -1.0).astype(F32)
    tables = {}
    for block, ref in zip(blocks, leg_refs):
        turned = ref[0].T
        tables[block, False] = turned
        tables[block, True] = turned * sign
    total = None
    for i, row in enumerate(chunk):
        parts = [
            arrived_ref[pl.ds((slot * rows + i) * QB + b, DEVICES, stride=SLOTS * rows * QB), :]
            for b in range(QB)
        ]
        weights = jnp.concatenate(
            [weight_ref[block * BLOCK : (block + 1) * BLOCK, :] for block, _ in row], axis=0
        )
        values = jnp.concatenate(parts, axis=1) * weights
        table = jnp.concatenate([tables[piece] for piece in row], axis=1)
        term = dot3(split(table), split(values))
        total = term if total is None else total + term
    total = jnp.where(degrees >= wave, total, 0.0)
    if partial:
        total = total + refs[len(blocks)][0]
    out_ref[0] = total


def analyse(chunk, own_waves, arrived, weights, legendre, partial=None):
    blocks = blocks_of(chunk)
    rows = len(chunk)
    slab = pl.BlockSpec((1, M, 2 * C), lambda s: (s, 0, 0))
    return pl.pallas_call(
        functools.partial(analyse_kernel, chunk, partial is not None),
        out_shape=jax.ShapeDtypeStruct((SLOTS, M, 2 * C), F32),
        grid=(SLOTS,),
        in_specs=[
            pl.BlockSpec(memory_space=pltpu.SMEM),
            pl.BlockSpec(arrived.shape, lambda s: (0, 0)),
            pl.BlockSpec(weights.shape, lambda s: (0, 0)),
        ]
        + [pl.BlockSpec((1, BLOCK, M), lambda s, k=k: (s, k, 0)) for k in blocks]
        + ([] if partial is None else [slab]),
        out_specs=slab,
        compiler_params=pltpu.CompilerParams(vmem_limit_bytes=VMEM_LIMIT),
        cost_estimate=pl.CostEstimate(
            flops=6 * SLOTS * DEVICES * rows * M * 2 * C,
            bytes_accessed=4 * (SLOTS * M * 2 * C * 2 + arrived.size),
            transcendentals=0,
        ),
        name="legendre_analysis",
    )(
        own_waves,
        arrived,
        weights,
        *([legendre] * len(blocks)),
        *(() if partial is None else (partial,)),
    )


def exchange(flat, rows):
    pieces = flat.reshape(DEVICES, SLOTS * rows, QB, LANES)
    moved = lax.all_to_all(pieces, AXES, split_axis=0, concat_axis=0, tiled=True)
    return moved.reshape(flat.shape)


def fourier_tables(wave_table):
    longitudes = jnp.arange(KPAD, dtype=jnp.int32)

    def table(waves, lons):
        angles = (waves * lons % NLON).astype(F32) * (2.0 * math.pi / NLON)
        return jnp.cos(angles), jnp.sin(angles)

    amplitude = jnp.where(wave_table == 0, 1.0, 2.0).astype(F32)[None, :]
    cosines, sines = table(wave_table[None, :], longitudes[:, None])
    share = jnp.where(
        longitudes > NLON // 2,
        0.0,
        jnp.where((longitudes == 0) | (longitudes == NLON // 2), 0.5, 1.0),
    ).astype(F32)[None, :] * (1.0 / NLON)
    back_cosines, back_sines = table(wave_table[:, None], longitudes[None, :])
    return cosines * amplitude, sines * amplitude, back_cosines * share, -back_sines * share


def body(spectrum, legendre, wave_table, quad_weight, norm_gain, weight_in, bias_in, weight_out):
    device_index = lax.axis_index(AXES)
    own_waves = lax.dynamic_slice_in_dim(wave_table, device_index * SLOTS, SLOTS)
    weights = quad_weight[:, None]
    tables = fourier_tables(wave_table)
    gain, bias = norm_gain[None, :], bias_in[None, :]
    arrived = [
        exchange(synth(chunk, own_waves, spectrum, legendre), len(chunk)) for chunk in CHUNKS
    ]
    back = [
        exchange(
            physics(len(chunk), value, tables, gain, weight_in, bias, weight_out), len(chunk)
        )
        for chunk, value in zip(CHUNKS, arrived)
    ]
    total = None
    for chunk, value in zip(CHUNKS, back):
        total = analyse(chunk, own_waves, value, weights, legendre, total)
    return total


def solution(mesh):
    return jax.shard_map(
        body,
        mesh=mesh,
        in_specs=(P(AXES, None, None), P(AXES, None, None), P(), P(), P(), P(), P(), P()),
        out_specs=P(AXES, None, None),
        check_vma=False,
    )
```

```python
import functools
import math

import jax
import jax.numpy as jnp
from jax import lax
from jax.experimental import pallas as pl
from jax.experimental.pallas import tpu as pltpu
from jax.sharding import PartitionSpec as P

M = 640
C = 256
HALF = 320
NLON = 1280
HIDDEN = 512
DEVICES = 128
SLOTS = M // DEVICES
LANES = 128
QB = 2 * C // LANES
BLOCK = 64
KPAD = 672
KBLOCKS = 2
KB = KPAD // KBLOCKS
AHEAD = 3
AXES = ("lat", "lon")
MIB = 1024 * 1024
F32 = jnp.float32
BF16 = jnp.bfloat16

CHUNKS = (
    (((0, False), (1, False)), ((0, True), (1, True))),
    (((2, False), (3, False)), ((2, True), (3, True)), ((4, False), (4, True))),
)


def blocks_of(chunk):
    return sorted({block for row in chunk for block, _ in row})


def span_of(chunk):
    blocks = blocks_of(chunk)
    return blocks[0] * BLOCK, len(blocks) * BLOCK


def own_wave(waves_ref, slot):
    return waves_ref[lax.axis_index(AXES) * SLOTS + slot]


def split(value):
    high = value.astype(BF16)
    low = (value - high.astype(F32)).astype(BF16)
    return high, low


def across3(value):
    high, low = split(value)
    return jnp.concatenate([high, high, low], axis=1)


def down3(value):
    high, low = split(value)
    return jnp.concatenate([high, low, high], axis=0)


def dot(left, right):
    return jnp.dot(left, right, preferred_element_type=F32)


def start(copies, source, target, semaphore):
    copy = pltpu.make_async_copy(source, target, semaphore)
    copy.start()
    copies.append(copy)


def synth_kernel(
    chunk, waves_ref, spec_hbm, leg_hbm, out_hbm, spec, leg, out, spec_sem, leg_sem, out_sem
):
    rows = len(chunk)
    first, count = span_of(chunk)
    blocks = blocks_of(chunk)
    by_slot = out.ndim > 2
    spec_in, leg_in, sent = [], [], []

    def fetch(s):
        if s < SLOTS:
            start(leg_in, leg_hbm.at[s, pl.ds(first, count), :], leg.at[s], leg_sem.at[s])
            start(spec_in, spec_hbm.at[s], spec.at[s], spec_sem.at[s])

    for s in range(AHEAD):
        fetch(s)
    across = lax.broadcasted_iota(jnp.int32, (1, M), 1)
    for s in range(SLOTS):
        fetch(s + AHEAD)
        wave = own_wave(waves_ref, s)
        keep = jnp.where(across >= wave, 1.0, 0.0).astype(F32)
        sign = jnp.where((across + wave) % 2 == 0, 1.0, -1.0).astype(BF16)
        leg_in[s].wait()
        parts = {}
        for j, block in enumerate(blocks):
            table = across3(leg[s, j * BLOCK : (j + 1) * BLOCK, :] * keep)
            parts[block, False] = table
            parts[block, True] = table * jnp.concatenate([sign] * 3, axis=1)
        left = jnp.concatenate([parts[piece] for row in chunk for piece in row], axis=0)
        spec_in[s].wait()
        fourier = dot(left, down3(spec[s]))
        if by_slot:
            flat, begin, stride = out.at[s].reshape(DEVICES * rows * QB, LANES), 0, rows * QB
        else:
            flat, begin, stride = out, s * rows * QB, SLOTS * rows * QB
        for i in range(rows):
            for b in range(QB):
                part = fourier[i * DEVICES : (i + 1) * DEVICES, b * LANES : (b + 1) * LANES]
                if b >= QB // 2:
                    part = jnp.where(wave > 0, part, 0.0)
                flat[pl.ds(begin + i * QB + b, DEVICES, stride=stride), :] = part
        if by_slot:
            start(sent, out.at[s], out_hbm.at[:, s], out_sem.at[s])
    if not by_slot:
        start(sent, out, out_hbm, out_sem.at[0])
    for copy in sent:
        copy.wait()


def synth(chunk, waves, spectrum, legendre):
    rows = len(chunk)
    count = span_of(chunk)[1]
    if rows * QB % 8 == 0:
        shape = (DEVICES, SLOTS, rows * QB, LANES)
        buffer = (SLOTS, DEVICES, rows * QB, LANES)
    else:
        shape = buffer = (DEVICES * SLOTS * rows * QB, LANES)
    hbm = pl.BlockSpec(memory_space=pltpu.HBM)
    return pl.pallas_call(
        functools.partial(synth_kernel, chunk),
        out_shape=jax.ShapeDtypeStruct(shape, F32),
        in_specs=[pl.BlockSpec(memory_space=pltpu.SMEM), hbm, hbm],
        out_specs=hbm,
        scratch_shapes=[
            pltpu.VMEM((SLOTS, M, 2 * C), F32),
            pltpu.VMEM((SLOTS, count, M), F32),
            pltpu.VMEM(buffer, F32),
        ]
        + [pltpu.SemaphoreType.DMA((SLOTS,))] * 3,
        compiler_params=pltpu.CompilerParams(vmem_limit_bytes=63 * MIB),
        cost_estimate=pl.CostEstimate(
            flops=6 * SLOTS * DEVICES * rows * M * 2 * C,
            bytes_accessed=4 * SLOTS * (2 * M * C + count * M + DEVICES * rows * 2 * C),
            transcendentals=0,
        ),
        name="legendre_synthesis",
    )(waves, spectrum, legendre)


def tables_kernel(waves_ref, cos_ref, sin_ref, syn_ref, ana_ref):
    amplitude = jnp.where(waves_ref[...] == 0, 1.0, 2.0).astype(F32)
    longitudes = lax.broadcasted_iota(jnp.int32, (1, KPAD), 1)
    edge = (longitudes == 0) | (longitudes == NLON // 2)
    share = jnp.where(longitudes > NLON // 2, 0.0, jnp.where(edge, 0.5, 1.0) / NLON).astype(F32)
    for j, ref in enumerate((cos_ref, sin_ref)):
        table = ref[...]
        syn_ref[2 * j], syn_ref[2 * j + 1] = split(table.T * amplitude)
        ana_ref[2 * j], ana_ref[2 * j + 1] = split(table * (share if j == 0 else -share))


def fourier_tables(wave_table):
    longitudes = jnp.arange(KPAD, dtype=jnp.int32)
    angles = (wave_table[:, None] * longitudes[None, :] % NLON).astype(F32) * (2.0 * math.pi / NLON)
    return pl.pallas_call(
        tables_kernel,
        out_shape=(
            jax.ShapeDtypeStruct((4, KPAD, M), BF16),
            jax.ShapeDtypeStruct((4, M, KPAD), BF16),
        ),
        compiler_params=pltpu.CompilerParams(vmem_limit_bytes=48 * MIB),
        name="fourier_tables",
    )(wave_table[None, :], jnp.cos(angles), jnp.sin(angles))


def physics_kernel(
    rows,
    x_ref,
    syn_ref,
    ana_ref,
    gain_ref,
    win_ref,
    bias_ref,
    wout_ref,
    out_ref,
    w1_ref,
    w2_ref,
    tend_ref,
):
    row = pl.program_id(0)

    @pl.when(row == 0)
    def _():
        w1_ref[...] = down3(win_ref[...])
        w2_ref[...] = down3(wout_ref[...])

    step = rows * QB
    parts = [x_ref[pl.ds(row * QB + b, M, stride=step), :] for b in range(QB)]
    real = down3(jnp.concatenate(parts[: QB // 2], axis=1))
    imag = down3(jnp.concatenate(parts[QB // 2 :], axis=1))

    def table3(ref, j, rng):
        high, low = ref[2 * j, rng, :], ref[2 * j + 1, rng, :]
        return jnp.concatenate([high, high, low], axis=1)

    for k in range(KBLOCKS):
        rng = slice(k * KB, (k + 1) * KB)
        even = dot(table3(syn_ref, 0, rng), real)
        odd = dot(table3(syn_ref, 1, rng), imag)
        columns = jnp.concatenate([even - odd, even + odd], axis=0)
        mean_square = jnp.mean(columns * columns, axis=-1, keepdims=True)
        normed = columns * gain_ref[...] * lax.rsqrt(mean_square + 1e-06)
        hidden = dot(across3(normed), w1_ref[...]) + bias_ref[...]
        hidden = hidden / (1.0 + jnp.exp(-hidden))
        tendency = dot(across3(hidden), w2_ref[...])
        plus, minus = tendency[:KB], tendency[KB:]
        tend_ref[0, rng, :], tend_ref[1, rng, :] = split(plus + minus)
        tend_ref[2, rng, :], tend_ref[3, rng, :] = split(plus - minus)
    for j in range(2):
        high, low = tend_ref[2 * j], tend_ref[2 * j + 1]
        back = dot(table3(ana_ref, j, slice(0, M)), jnp.concatenate([high, low, high], axis=0))
        for h in range(QB // 2):
            part = back[:, h * LANES : (h + 1) * LANES]
            out_ref[pl.ds(row * QB + j * (QB // 2) + h, M, stride=step), :] = part


def physics(rows, arrived, tables, gain, weight_in, bias, weight_out):
    total = M * rows * QB
    whole = lambda shape: pl.BlockSpec(shape, lambda r: (0,) * len(shape))
    operands = (arrived, *tables, gain, weight_in, bias, weight_out)
    return pl.pallas_call(
        functools.partial(physics_kernel, rows),
        out_shape=jax.ShapeDtypeStruct((total, LANES), F32),
        grid=(rows,),
        in_specs=[whole(x.shape) for x in operands],
        out_specs=whole((total, LANES)),
        scratch_shapes=[
            pltpu.VMEM((3 * C, HIDDEN), BF16),
            pltpu.VMEM((3 * HIDDEN, C), BF16),
            pltpu.VMEM((4, KPAD, C), BF16),
        ],
        compiler_params=pltpu.CompilerParams(vmem_limit_bytes=63 * MIB),
        cost_estimate=pl.CostEstimate(
            flops=6 * rows * KPAD * (4 * M * C + 4 * C * HIDDEN),
            bytes_accessed=8 * total * LANES + 16 * KPAD * M,
            transcendentals=2 * rows * KPAD * HIDDEN,
        ),
        name="column_physics",
    )(*operands)


def turn_kernel(waves_ref, weight_ref, *refs):
    leg_refs, out_ref, turned = refs[:-2], refs[-2], refs[-1]
    wave = own_wave(waves_ref, pl.program_id(0))
    degrees = lax.broadcasted_iota(jnp.int32, (M, 1), 0)
    keep = jnp.where(degrees >= wave, 1.0, 0.0).astype(F32)
    count = weight_ref.shape[0]
    rows = jnp.concatenate([ref[0] for ref in leg_refs], axis=0) * weight_ref[...]
    if count % LANES:
        rows = jnp.concatenate([rows, jnp.zeros((LANES - count % LANES, M), F32)], axis=0)
    table = rows.T * keep
    for j in range(turned.shape[0]):
        turned[j] = table[:, j * LANES : (j + 1) * LANES]
    for parity in range(2):
        half = [
            turned.at[j][pl.ds(parity, M // 2, stride=2), :] for j in range(turned.shape[0])
        ]
        out_ref[0, parity] = jnp.concatenate(
            split(jnp.concatenate(half, axis=1)[:, :count]), axis=1
        )


def turn(chunk, waves, weights, legendre):
    first, count = span_of(chunk)
    shape = (1, 2, M // 2, 2 * count)
    return pl.pallas_call(
        turn_kernel,
        out_shape=jax.ShapeDtypeStruct((SLOTS,) + shape[1:], BF16),
        grid=(SLOTS,),
        in_specs=[
            pl.BlockSpec(memory_space=pltpu.SMEM),
            pl.BlockSpec((count, 1), lambda s: (0, 0)),
        ]
        + [pl.BlockSpec((1, BLOCK, M), lambda s, k=k: (s, k, 0)) for k in blocks_of(chunk)],
        out_specs=pl.BlockSpec(shape, lambda s: (s, 0, 0, 0)),
        scratch_shapes=[pltpu.VMEM((-(-count // LANES), M, LANES), F32)],
        compiler_params=pltpu.CompilerParams(vmem_limit_bytes=48 * MIB),
        name="turned_tables",
    )(waves, weights[first : first + count], *([legendre] * len(blocks_of(chunk))))


def analyse_kernel(chunk, last, waves_ref, arrived_hbm, table_hbm, *refs):
    if last:
        partial_hbm, out_hbm, arrived, table, in_sem, table_sem, partial, part_sem, out, out_sem = refs
    else:
        out_hbm, arrived, table, in_sem, table_sem, out, out_sem = refs
    rows = len(chunk)
    count = span_of(chunk)[1]
    blocks = blocks_of(chunk)
    came, tables, partials, sent = [], [], [], []

    def fetch(s):
        if s < SLOTS:
            start(came, arrived_hbm.at[:, s], arrived.at[s], in_sem.at[s])
            start(tables, table_hbm.at[s], table.at[s], table_sem.at[s])
            if last:
                start(partials, partial_hbm.at[s], partial.at[s], part_sem.at[s])

    for s in range(AHEAD):
        fetch(s)
    for s in range(SLOTS):
        fetch(s + AHEAD)
        wave = own_wave(waves_ref, s)
        came[s].wait()
        flat = arrived.at[s].reshape(DEVICES * rows * QB, LANES)
        values = [
            jnp.concatenate(
                [flat[pl.ds(i * QB + b, DEVICES, stride=rows * QB), :] for b in range(QB)], axis=1
            )
            for i in range(rows)
        ]
        halves = {
            piece: values[i][h * BLOCK : (h + 1) * BLOCK]
            for i, row in enumerate(chunk)
            for h, piece in enumerate(row)
        }
        north = jnp.concatenate([halves[k, False] for k in blocks], axis=0)
        south = jnp.concatenate([halves[k, True] for k in blocks], axis=0)
        tables[s].wait()
        if last:
            partials[s].wait()
        for parity in range(2):
            sign = jnp.where((wave + parity) % 2 == 0, 1.0, -1.0).astype(F32)
            high, low = split(north + sign * south)
            left = table.at[s, parity]
            term = dot(left[...], jnp.concatenate([high, high], axis=0))
            term = term + dot(left[:, :count], low)
            if last:
                term = term + partial[s, parity]
                for b in range(QB):
                    out.at[s, b][pl.ds(parity, M // 2, stride=2), :] = (
                        term[:, b * LANES : (b + 1) * LANES]
                    )
            else:
                out[s, parity] = term
        if last:
            for b in range(QB):
                target = out_hbm.at[s, :, b * LANES : (b + 1) * LANES]
                start(sent, out.at[s, b], target, out_sem.at[s, b])
        else:
            start(sent, out.at[s], out_hbm.at[s], out_sem.at[s, 0])
    for copy in sent:
        copy.wait()


def analyse(chunk, waves, arrived, table, partial=None):
    rows = len(chunk)
    last = partial is not None
    tail = (rows * QB, LANES) if rows * QB % 8 == 0 else (rows, QB, LANES)
    split_shape = (SLOTS, 2, M // 2, 2 * C)
    shape = (SLOTS, M, 2 * C) if last else split_shape
    hbm = pl.BlockSpec(memory_space=pltpu.HBM)
    semaphores = pltpu.SemaphoreType.DMA((SLOTS,))
    return pl.pallas_call(
        functools.partial(analyse_kernel, chunk, last),
        out_shape=jax.ShapeDtypeStruct(shape, F32),
        in_specs=[pl.BlockSpec(memory_space=pltpu.SMEM), hbm, hbm] + [hbm] * last,
        out_specs=hbm,
        scratch_shapes=[
            pltpu.VMEM((SLOTS, DEVICES) + tail, F32),
            pltpu.VMEM(table.shape, BF16),
            semaphores,
            semaphores,
        ]
        + [pltpu.VMEM(split_shape, F32), semaphores] * last
        + [
            pltpu.VMEM((SLOTS, QB, M, LANES) if last else shape, F32),
            pltpu.SemaphoreType.DMA((SLOTS, QB)),
        ],
        compiler_params=pltpu.CompilerParams(vmem_limit_bytes=63 * MIB),
        cost_estimate=pl.CostEstimate(
            flops=3 * SLOTS * DEVICES * rows * M * 2 * C,
            bytes_accessed=4 * (SLOTS * M * 2 * C * 2 + arrived.size),
            transcendentals=0,
        ),
        name="legendre_analysis",
    )(waves, arrived.reshape((DEVICES, SLOTS) + tail), table, *((partial,) if last else ()))


def exchange(value, rows):
    pieces = value.reshape(DEVICES, SLOTS * rows, QB, LANES)
    moved = lax.all_to_all(pieces, AXES, split_axis=0, concat_axis=0, tiled=True)
    return moved.reshape(M * rows * QB, LANES)


def body(spectrum, legendre, wave_table, quad_weight, norm_gain, weight_in, bias_in, weight_out):
    weights = quad_weight[:, None]
    gain, bias = norm_gain[None, :], bias_in[None, :]
    tables = fourier_tables(wave_table)
    turned = [turn(chunk, wave_table, weights, legendre) for chunk in CHUNKS]
    arrived = [
        exchange(synth(chunk, wave_table, spectrum, legendre), len(chunk)) for chunk in CHUNKS
    ]
    back = [
        exchange(
            physics(len(chunk), value, tables, gain, weight_in, bias, weight_out), len(chunk)
        )
        for chunk, value in zip(CHUNKS, arrived)
    ]
    total = None
    for chunk, value, table in zip(CHUNKS, back, turned):
        total = analyse(chunk, wave_table, value, table, total)
    return total


def solution(mesh):
    return jax.shard_map(
        body,
        mesh=mesh,
        in_specs=(P(AXES, None, None), P(AXES, None, None), P(), P(), P(), P(), P(), P()),
        out_specs=P(AXES, None, None),
        check_vma=False,
    )
```

```python
import functools
import math

import jax
import jax.numpy as jnp
from jax import lax
from jax.experimental import pallas as pl
from jax.experimental.pallas import tpu as pltpu
from jax.sharding import PartitionSpec as P

M = 640
C = 256
HALF = 320
NLON = 1280
HIDDEN = 512
DEVICES = 128
SLOTS = M // DEVICES
LANES = 128
QB = 2 * C // LANES
BLOCK = 64
KPAD = 672
KBLOCKS = 2
KB = KPAD // KBLOCKS
AHEAD = 3
AXES = ("lat", "lon")
MIB = 1024 * 1024
F32 = jnp.float32
BF16 = jnp.bfloat16

CHUNKS = (
    (((0, False), (1, False)), ((0, True), (1, True))),
    (((2, False), (3, False)), ((2, True), (3, True)), ((4, False), (4, True))),
)


def blocks_of(chunk):
    return sorted({block for row in chunk for block, _ in row})


def span_of(chunk):
    blocks = blocks_of(chunk)
    return blocks[0] * BLOCK, len(blocks) * BLOCK


def own_wave(waves_ref, slot):
    return waves_ref[lax.axis_index(AXES) * SLOTS + slot]


def split(value):
    high = value.astype(BF16)
    low = (value - high.astype(F32)).astype(BF16)
    return high, low


def across3(value):
    high, low = split(value)
    return jnp.concatenate([high, high, low], axis=1)


def down3(value):
    high, low = split(value)
    return jnp.concatenate([high, low, high], axis=0)


def dot(left, right):
    return jnp.dot(left, right, preferred_element_type=F32)


def each_slot(copies, work):
    def begin(s):
        for copy in copies(s):
            copy.start()

    def step(s, carry):
        pl.when(s + AHEAD < SLOTS)(lambda: begin(s + AHEAD))
        for copy in copies(s):
            copy.wait()
        work(s)
        return carry

    for s in range(AHEAD):
        begin(s)
    lax.fori_loop(0, SLOTS, step, 0)


def synth_kernel(
    chunk, waves_ref, spec_hbm, leg_hbm, out_hbm, spec, leg, out, spec_sem, leg_sem, out_sem
):
    rows = len(chunk)
    first, count = span_of(chunk)
    blocks = blocks_of(chunk)
    by_slot = out.ndim > 2
    across = lax.broadcasted_iota(jnp.int32, (1, M), 1)

    def fetched(s):
        return (
            pltpu.make_async_copy(
                leg_hbm.at[s, pl.ds(first, count), :], leg.at[s], leg_sem.at[s]
            ),
            pltpu.make_async_copy(spec_hbm.at[s], spec.at[s], spec_sem.at[s]),
        )

    def sent(s):
        if by_slot:
            return pltpu.make_async_copy(out.at[s], out_hbm.at[:, s], out_sem.at[s])
        return pltpu.make_async_copy(out, out_hbm, out_sem.at[0])

    def work(s):
        wave = own_wave(waves_ref, s)
        keep = jnp.where(across >= wave, 1.0, 0.0).astype(F32)
        sign = jnp.where((across + wave) % 2 == 0, 1.0, -1.0).astype(BF16)
        sign = jnp.concatenate([sign] * 3, axis=1)
        parts = {}
        for j, block in enumerate(blocks):
            table = across3(leg[s, j * BLOCK : (j + 1) * BLOCK, :] * keep)
            parts[block, False] = table
            parts[block, True] = table * sign
        left = jnp.concatenate([parts[piece] for row in chunk for piece in row], axis=0)
        fourier = dot(left, down3(spec[s]))
        if by_slot:
            flat, begin, stride = out.at[s].reshape(DEVICES * rows * QB, LANES), 0, rows * QB
        else:
            flat, begin, stride = out, s * rows * QB, SLOTS * rows * QB
        for i in range(rows):
            for b in range(QB):
                part = fourier[i * DEVICES : (i + 1) * DEVICES, b * LANES : (b + 1) * LANES]
                if b >= QB // 2:
                    part = jnp.where(wave > 0, part, 0.0)
                flat[pl.ds(begin + i * QB + b, DEVICES, stride=stride), :] = part
        if by_slot:
            sent(s).start()

    each_slot(fetched, work)
    if not by_slot:
        sent(0).start()
    for s in range(SLOTS if by_slot else 1):
        sent(s).wait()


def synth(chunk, waves, spectrum, legendre):
    rows = len(chunk)
    count = span_of(chunk)[1]
    if rows * QB % 8 == 0:
        shape = (DEVICES, SLOTS, rows * QB, LANES)
        buffer = (SLOTS, DEVICES, rows * QB, LANES)
    else:
        shape = buffer = (DEVICES * SLOTS * rows * QB, LANES)
    hbm = pl.BlockSpec(memory_space=pltpu.HBM)
    return pl.pallas_call(
        functools.partial(synth_kernel, chunk),
        out_shape=jax.ShapeDtypeStruct(shape, F32),
        in_specs=[pl.BlockSpec(memory_space=pltpu.SMEM), hbm, hbm],
        out_specs=hbm,
        scratch_shapes=[
            pltpu.VMEM((SLOTS, M, 2 * C), F32),
            pltpu.VMEM((SLOTS, count, M), F32),
            pltpu.VMEM(buffer, F32),
        ]
        + [pltpu.SemaphoreType.DMA((SLOTS,))] * 3,
        compiler_params=pltpu.CompilerParams(vmem_limit_bytes=63 * MIB),
        cost_estimate=pl.CostEstimate(
            flops=6 * SLOTS * DEVICES * rows * M * 2 * C,
            bytes_accessed=4 * SLOTS * (2 * M * C + count * M + DEVICES * rows * 2 * C),
            transcendentals=0,
        ),
        name="legendre_synthesis",
    )(waves, spectrum, legendre)


def tables_kernel(waves_ref, cos_ref, sin_ref, syn_ref, ana_ref):
    amplitude = jnp.where(waves_ref[...] == 0, 1.0, 2.0).astype(F32)
    longitudes = lax.broadcasted_iota(jnp.int32, (1, KPAD), 1)
    edge = (longitudes == 0) | (longitudes == NLON // 2)
    share = jnp.where(longitudes > NLON // 2, 0.0, jnp.where(edge, 0.5, 1.0) / NLON).astype(F32)
    for j, ref in enumerate((cos_ref, sin_ref)):
        table = ref[...]
        syn_ref[2 * j], syn_ref[2 * j + 1] = split(table.T * amplitude)
        ana_ref[2 * j], ana_ref[2 * j + 1] = split(table * (share if j == 0 else -share))


def fourier_tables(wave_table):
    longitudes = jnp.arange(KPAD, dtype=jnp.int32)
    angles = (wave_table[:, None] * longitudes[None, :] % NLON).astype(F32) * (2.0 * math.pi / NLON)
    return pl.pallas_call(
        tables_kernel,
        out_shape=(
            jax.ShapeDtypeStruct((4, KPAD, M), BF16),
            jax.ShapeDtypeStruct((4, M, KPAD), BF16),
        ),
        compiler_params=pltpu.CompilerParams(vmem_limit_bytes=48 * MIB),
        name="fourier_tables",
    )(wave_table[None, :], jnp.cos(angles), jnp.sin(angles))


def physics_kernel(
    rows,
    x_ref,
    syn_ref,
    ana_ref,
    gain_ref,
    win_ref,
    bias_ref,
    wout_ref,
    out_ref,
    w1_ref,
    w2_ref,
    tend_ref,
):
    row = pl.program_id(0)

    @pl.when(row == 0)
    def _():
        w1_ref[...] = down3(win_ref[...])
        w2_ref[...] = down3(wout_ref[...])

    step = rows * QB
    parts = [x_ref[pl.ds(row * QB + b, M, stride=step), :] for b in range(QB)]
    real = down3(jnp.concatenate(parts[: QB // 2], axis=1))
    imag = down3(jnp.concatenate(parts[QB // 2 :], axis=1))

    def table3(ref, j, rng):
        high, low = ref[2 * j, rng, :], ref[2 * j + 1, rng, :]
        return jnp.concatenate([high, high, low], axis=1)

    def longitudes(k, carry):
        rng = pl.ds(pl.multiple_of(k * KB, KB), KB)
        even = dot(table3(syn_ref, 0, rng), real)
        odd = dot(table3(syn_ref, 1, rng), imag)
        columns = jnp.concatenate([even - odd, even + odd], axis=0)
        mean_square = jnp.mean(columns * columns, axis=-1, keepdims=True)
        normed = columns * gain_ref[...] * lax.rsqrt(mean_square + 1e-06)
        hidden = dot(across3(normed), w1_ref[...]) + bias_ref[...]
        hidden = hidden / (1.0 + jnp.exp(-hidden))
        tendency = dot(across3(hidden), w2_ref[...])
        plus, minus = tendency[:KB], tendency[KB:]
        tend_ref[0, rng, :], tend_ref[1, rng, :] = split(plus + minus)
        tend_ref[2, rng, :], tend_ref[3, rng, :] = split(plus - minus)
        return carry

    lax.fori_loop(0, KBLOCKS, longitudes, 0)
    for j in range(2):
        high, low = tend_ref[2 * j], tend_ref[2 * j + 1]
        back = dot(table3(ana_ref, j, slice(0, M)), jnp.concatenate([high, low, high], axis=0))
        for h in range(QB // 2):
            part = back[:, h * LANES : (h + 1) * LANES]
            out_ref[pl.ds(row * QB + j * (QB // 2) + h, M, stride=step), :] = part


def physics(rows, arrived, tables, gain, weight_in, bias, weight_out):
    total = M * rows * QB
    whole = lambda shape: pl.BlockSpec(shape, lambda r: (0,) * len(shape))
    operands = (arrived, *tables, gain, weight_in, bias, weight_out)
    return pl.pallas_call(
        functools.partial(physics_kernel, rows),
        out_shape=jax.ShapeDtypeStruct((total, LANES), F32),
        grid=(rows,),
        in_specs=[whole(x.shape) for x in operands],
        out_specs=whole((total, LANES)),
        scratch_shapes=[
            pltpu.VMEM((3 * C, HIDDEN), BF16),
            pltpu.VMEM((3 * HIDDEN, C), BF16),
            pltpu.VMEM((4, KPAD, C), BF16),
        ],
        compiler_params=pltpu.CompilerParams(vmem_limit_bytes=63 * MIB),
        cost_estimate=pl.CostEstimate(
            flops=6 * rows * KPAD * (4 * M * C + 4 * C * HIDDEN),
            bytes_accessed=8 * total * LANES + 16 * KPAD * M,
            transcendentals=2 * rows * KPAD * HIDDEN,
        ),
        name="column_physics",
    )(*operands)


def turn_kernel(waves_ref, weight_ref, *refs):
    leg_refs, out_ref, turned = refs[:-2], refs[-2], refs[-1]
    wave = own_wave(waves_ref, pl.program_id(0))
    degrees = lax.broadcasted_iota(jnp.int32, (M, 1), 0)
    keep = jnp.where(degrees >= wave, 1.0, 0.0).astype(F32)
    count = weight_ref.shape[0]
    rows = jnp.concatenate([ref[0] for ref in leg_refs], axis=0) * weight_ref[...]
    if count % LANES:
        rows = jnp.concatenate([rows, jnp.zeros((LANES - count % LANES, M), F32)], axis=0)
    table = rows.T * keep
    for j in range(turned.shape[0]):
        turned[j] = table[:, j * LANES : (j + 1) * LANES]
    for parity in range(2):
        half = [
            turned.at[j][pl.ds(parity, M // 2, stride=2), :] for j in range(turned.shape[0])
        ]
        out_ref[0, parity] = jnp.concatenate(
            split(jnp.concatenate(half, axis=1)[:, :count]), axis=1
        )


def turn(chunk, waves, weights, legendre):
    first, count = span_of(chunk)
    shape = (1, 2, M // 2, 2 * count)
    return pl.pallas_call(
        turn_kernel,
        out_shape=jax.ShapeDtypeStruct((SLOTS,) + shape[1:], BF16),
        grid=(SLOTS,),
        in_specs=[
            pl.BlockSpec(memory_space=pltpu.SMEM),
            pl.BlockSpec((count, 1), lambda s: (0, 0)),
        ]
        + [pl.BlockSpec((1, BLOCK, M), lambda s, k=k: (s, k, 0)) for k in blocks_of(chunk)],
        out_specs=pl.BlockSpec(shape, lambda s: (s, 0, 0, 0)),
        scratch_shapes=[pltpu.VMEM((-(-count // LANES), M, LANES), F32)],
        compiler_params=pltpu.CompilerParams(vmem_limit_bytes=48 * MIB),
        name="turned_tables",
    )(waves, weights[first : first + count], *([legendre] * len(blocks_of(chunk))))


def analyse_kernel(chunk, last, waves_ref, arrived_hbm, table_hbm, *refs):
    if last:
        partial_hbm, out_hbm, arrived, table, in_sem, table_sem, partial, part_sem, out, out_sem = refs
    else:
        out_hbm, arrived, table, in_sem, table_sem, out, out_sem = refs
    rows = len(chunk)
    count = span_of(chunk)[1]
    blocks = blocks_of(chunk)

    def fetched(s):
        copies = [
            pltpu.make_async_copy(arrived_hbm.at[:, s], arrived.at[s], in_sem.at[s]),
            pltpu.make_async_copy(table_hbm.at[s], table.at[s], table_sem.at[s]),
        ]
        if last:
            copies.append(pltpu.make_async_copy(partial_hbm.at[s], partial.at[s], part_sem.at[s]))
        return copies

    def sent(s):
        if not last:
            return [pltpu.make_async_copy(out.at[s], out_hbm.at[s], out_sem.at[s, 0])]
        return [
            pltpu.make_async_copy(
                out.at[s, b], out_hbm.at[s, :, b * LANES : (b + 1) * LANES], out_sem.at[s, b]
            )
            for b in range(QB)
        ]

    def work(s):
        wave = own_wave(waves_ref, s)
        flat = arrived.at[s].reshape(DEVICES * rows * QB, LANES)
        values = [
            jnp.concatenate(
                [flat[pl.ds(i * QB + b, DEVICES, stride=rows * QB), :] for b in range(QB)], axis=1
            )
            for i in range(rows)
        ]
        halves = {
            piece: values[i][h * BLOCK : (h + 1) * BLOCK]
            for i, row in enumerate(chunk)
            for h, piece in enumerate(row)
        }
        north = jnp.concatenate([halves[k, False] for k in blocks], axis=0)
        south = jnp.concatenate([halves[k, True] for k in blocks], axis=0)
        for parity in range(2):
            sign = jnp.where((wave + parity) % 2 == 0, 1.0, -1.0).astype(F32)
            high, low = split(north + sign * south)
            left = table.at[s, parity]
            term = dot(left[...], jnp.concatenate([high, high], axis=0))
            term = term + dot(left[:, :count], low)
            if last:
                term = term + partial[s, parity]
                for b in range(QB):
                    out.at[s, b][pl.ds(parity, M // 2, stride=2), :] = (
                        term[:, b * LANES : (b + 1) * LANES]
                    )
            else:
                out[s, parity] = term
        for copy in sent(s):
            copy.start()

    each_slot(fetched, work)
    for s in range(SLOTS):
        for copy in sent(s):
            copy.wait()


def analyse(chunk, waves, arrived, table, partial=None):
    rows = len(chunk)
    last = partial is not None
    tail = (rows * QB, LANES) if rows * QB % 8 == 0 else (rows, QB, LANES)
    split_shape = (SLOTS, 2, M // 2, 2 * C)
    shape = (SLOTS, M, 2 * C) if last else split_shape
    hbm = pl.BlockSpec(memory_space=pltpu.HBM)
    semaphores = pltpu.SemaphoreType.DMA((SLOTS,))
    return pl.pallas_call(
        functools.partial(analyse_kernel, chunk, last),
        out_shape=jax.ShapeDtypeStruct(shape, F32),
        in_specs=[pl.BlockSpec(memory_space=pltpu.SMEM), hbm, hbm] + [hbm] * last,
        out_specs=hbm,
        scratch_shapes=[
            pltpu.VMEM((SLOTS, DEVICES) + tail, F32),
            pltpu.VMEM(table.shape, BF16),
            semaphores,
            semaphores,
        ]
        + [pltpu.VMEM(split_shape, F32), semaphores] * last
        + [
            pltpu.VMEM((SLOTS, QB, M, LANES) if last else shape, F32),
            pltpu.SemaphoreType.DMA((SLOTS, QB)),
        ],
        compiler_params=pltpu.CompilerParams(vmem_limit_bytes=63 * MIB),
        cost_estimate=pl.CostEstimate(
            flops=3 * SLOTS * DEVICES * rows * M * 2 * C,
            bytes_accessed=4 * (SLOTS * M * 2 * C * 2 + arrived.size),
            transcendentals=0,
        ),
        name="legendre_analysis",
    )(waves, arrived.reshape((DEVICES, SLOTS) + tail), table, *((partial,) if last else ()))


def exchange(value, rows):
    pieces = value.reshape(DEVICES, SLOTS * rows, QB, LANES)
    moved = lax.all_to_all(pieces, AXES, split_axis=0, concat_axis=0, tiled=True)
    return moved.reshape(M * rows * QB, LANES)


def body(spectrum, legendre, wave_table, quad_weight, norm_gain, weight_in, bias_in, weight_out):
    weights = quad_weight[:, None]
    gain, bias = norm_gain[None, :], bias_in[None, :]
    tables = fourier_tables(wave_table)
    turned = [turn(chunk, wave_table, weights, legendre) for chunk in CHUNKS]
    arrived = [
        exchange(synth(chunk, wave_table, spectrum, legendre), len(chunk)) for chunk in CHUNKS
    ]
    back = [
        exchange(
            physics(len(chunk), value, tables, gain, weight_in, bias, weight_out), len(chunk)
        )
        for chunk, value in zip(CHUNKS, arrived)
    ]
    total = None
    for chunk, value, table in zip(CHUNKS, back, turned):
        total = analyse(chunk, wave_table, value, table, total)
    return total


def solution(mesh):
    return jax.shard_map(
        body,
        mesh=mesh,
        in_specs=(P(AXES, None, None), P(AXES, None, None), P(), P(), P(), P(), P(), P()),
        out_specs=P(AXES, None, None),
        check_vma=False,
    )
```

```python
import functools
import math

import jax
import jax.numpy as jnp
from jax import lax
from jax.experimental import pallas as pl
from jax.experimental.pallas import tpu as pltpu
from jax.sharding import PartitionSpec as P

M = 640
C = 256
HALF = 320
NLON = 1280
HIDDEN = 512
DEVICES = 128
SLOTS = M // DEVICES
LANES = 128
QB = 2 * C // LANES
BLOCK = 64
KPAD = 672
KBLOCKS = 2
KB = KPAD // KBLOCKS
AHEAD = 3
AXES = ("lat", "lon")
MIB = 1024 * 1024
F32 = jnp.float32
BF16 = jnp.bfloat16

CHUNKS = (
    (((0, False), (1, False)), ((0, True), (1, True))),
    (((2, False), (3, False)), ((2, True), (3, True)), ((4, False), (4, True))),
)


def blocks_of(chunk):
    return sorted({block for row in chunk for block, _ in row})


def span_of(chunk):
    blocks = blocks_of(chunk)
    return blocks[0] * BLOCK, len(blocks) * BLOCK


def own_wave(waves_ref, slot):
    return waves_ref[lax.axis_index(AXES) * SLOTS + slot]


def split(value):
    high = value.astype(BF16)
    low = (value - high.astype(F32)).astype(BF16)
    return high, low


def across3(value):
    high, low = split(value)
    return jnp.concatenate([high, high, low], axis=1)


def down3(value):
    high, low = split(value)
    return jnp.concatenate([high, low, high], axis=0)


def dot(left, right):
    return jnp.dot(left, right, preferred_element_type=F32)


def each_slot(first, copies, work):
    def begin(s):
        for copy in copies(s):
            copy.start()

    def step(s, carry):
        pl.when(s + AHEAD < SLOTS)(lambda: begin(s + AHEAD))
        for copy in copies(s):
            copy.wait()
        work(s)
        return carry

    first.start()
    for s in range(AHEAD):
        begin(s)
    first.wait()
    lax.fori_loop(0, SLOTS, step, 0)


def synth_kernel(
    chunk,
    waves_hbm,
    spec_hbm,
    leg_hbm,
    out_hbm,
    waves_ref,
    waves_sem,
    spec,
    leg,
    out,
    spec_sem,
    leg_sem,
    out_sem,
):
    rows = len(chunk)
    first, count = span_of(chunk)
    blocks = blocks_of(chunk)
    by_slot = out.ndim > 2
    across = lax.broadcasted_iota(jnp.int32, (1, M), 1)

    def fetched(s):
        return (
            pltpu.make_async_copy(
                leg_hbm.at[s, pl.ds(first, count), :], leg.at[s], leg_sem.at[s]
            ),
            pltpu.make_async_copy(spec_hbm.at[s], spec.at[s], spec_sem.at[s]),
        )

    def sent(s):
        if by_slot:
            return pltpu.make_async_copy(out.at[s], out_hbm.at[:, s], out_sem.at[s])
        return pltpu.make_async_copy(out, out_hbm, out_sem.at[0])

    def work(s):
        wave = own_wave(waves_ref, s)
        keep = jnp.where(across >= wave, 1.0, 0.0).astype(F32)
        sign = jnp.where((across + wave) % 2 == 0, 1.0, -1.0).astype(BF16)
        sign = jnp.concatenate([sign] * 3, axis=1)
        parts = {}
        for j, block in enumerate(blocks):
            table = across3(leg[s, j * BLOCK : (j + 1) * BLOCK, :] * keep)
            parts[block, False] = table
            parts[block, True] = table * sign
        left = jnp.concatenate([parts[piece] for row in chunk for piece in row], axis=0)
        fourier = dot(left, down3(spec[s]))
        if by_slot:
            flat, begin, stride = out.at[s].reshape(DEVICES * rows * QB, LANES), 0, rows * QB
        else:
            flat, begin, stride = out, s * rows * QB, SLOTS * rows * QB
        for i in range(rows):
            for b in range(QB):
                part = fourier[i * DEVICES : (i + 1) * DEVICES, b * LANES : (b + 1) * LANES]
                if b >= QB // 2:
                    part = jnp.where(wave > 0, part, 0.0)
                flat[pl.ds(begin + i * QB + b, DEVICES, stride=stride), :] = part
        if by_slot:
            sent(s).start()

    each_slot(pltpu.make_async_copy(waves_hbm, waves_ref, waves_sem), fetched, work)
    if not by_slot:
        sent(0).start()
    for s in range(SLOTS if by_slot else 1):
        sent(s).wait()


def synth(chunk, waves, spectrum, legendre):
    rows = len(chunk)
    count = span_of(chunk)[1]
    if rows * QB % 8 == 0:
        shape = (DEVICES, SLOTS, rows * QB, LANES)
        buffer = (SLOTS, DEVICES, rows * QB, LANES)
    else:
        shape = buffer = (DEVICES * SLOTS * rows * QB, LANES)
    hbm = pl.BlockSpec(memory_space=pltpu.HBM)
    return pl.pallas_call(
        functools.partial(synth_kernel, chunk),
        out_shape=jax.ShapeDtypeStruct(shape, F32),
        in_specs=[hbm, hbm, hbm],
        out_specs=hbm,
        scratch_shapes=[
            pltpu.SMEM((M,), jnp.int32),
            pltpu.SemaphoreType.DMA,
            pltpu.VMEM((SLOTS, M, 2 * C), F32),
            pltpu.VMEM((SLOTS, count, M), F32),
            pltpu.VMEM(buffer, F32),
        ]
        + [pltpu.SemaphoreType.DMA((SLOTS,))] * 3,
        compiler_params=pltpu.CompilerParams(vmem_limit_bytes=63 * MIB),
        cost_estimate=pl.CostEstimate(
            flops=6 * SLOTS * DEVICES * rows * M * 2 * C,
            bytes_accessed=4 * SLOTS * (2 * M * C + count * M + DEVICES * rows * 2 * C),
            transcendentals=0,
        ),
        name="legendre_synthesis",
    )(waves, spectrum, legendre)


def tables_kernel(waves_ref, cos_ref, sin_ref, syn_ref, ana_ref):
    amplitude = jnp.where(waves_ref[...] == 0, 1.0, 2.0).astype(F32)
    longitudes = lax.broadcasted_iota(jnp.int32, (1, KPAD), 1)
    edge = (longitudes == 0) | (longitudes == NLON // 2)
    share = jnp.where(longitudes > NLON // 2, 0.0, jnp.where(edge, 0.5, 1.0) / NLON).astype(F32)
    for j, ref in enumerate((cos_ref, sin_ref)):
        table = ref[...]
        syn_ref[2 * j], syn_ref[2 * j + 1] = split(table.T * amplitude)
        ana_ref[2 * j], ana_ref[2 * j + 1] = split(table * (share if j == 0 else -share))


def fourier_tables(wave_table):
    longitudes = jnp.arange(KPAD, dtype=jnp.int32)
    angles = (wave_table[:, None] * longitudes[None, :] % NLON).astype(F32) * (2.0 * math.pi / NLON)
    return pl.pallas_call(
        tables_kernel,
        out_shape=(
            jax.ShapeDtypeStruct((4, KPAD, M), BF16),
            jax.ShapeDtypeStruct((4, M, KPAD), BF16),
        ),
        compiler_params=pltpu.CompilerParams(vmem_limit_bytes=48 * MIB),
        name="fourier_tables",
    )(wave_table[None, :], jnp.cos(angles), jnp.sin(angles))


def physics_kernel(
    rows,
    x_ref,
    syn_ref,
    ana_ref,
    gain_ref,
    win_ref,
    bias_ref,
    wout_ref,
    out_ref,
    w1_ref,
    w2_ref,
    tend_ref,
):
    row = pl.program_id(0)

    @pl.when(row == 0)
    def _():
        w1_ref[...] = down3(win_ref[...])
        w2_ref[...] = down3(wout_ref[...])

    step = rows * QB
    parts = [x_ref[pl.ds(row * QB + b, M, stride=step), :] for b in range(QB)]
    real = down3(jnp.concatenate(parts[: QB // 2], axis=1))
    imag = down3(jnp.concatenate(parts[QB // 2 :], axis=1))

    def table3(ref, j, rng):
        high, low = ref[2 * j, rng, :], ref[2 * j + 1, rng, :]
        return jnp.concatenate([high, high, low], axis=1)

    def longitudes(k, carry):
        rng = pl.ds(pl.multiple_of(k * KB, KB), KB)
        even = dot(table3(syn_ref, 0, rng), real)
        odd = dot(table3(syn_ref, 1, rng), imag)
        columns = jnp.concatenate([even - odd, even + odd], axis=0)
        mean_square = jnp.mean(columns * columns, axis=-1, keepdims=True)
        normed = columns * gain_ref[...] * lax.rsqrt(mean_square + 1e-06)
        hidden = dot(across3(normed), w1_ref[...]) + bias_ref[...]
        hidden = hidden / (1.0 + jnp.exp(-hidden))
        tendency = dot(across3(hidden), w2_ref[...])
        plus, minus = tendency[:KB], tendency[KB:]
        tend_ref[0, rng, :], tend_ref[1, rng, :] = split(plus + minus)
        tend_ref[2, rng, :], tend_ref[3, rng, :] = split(plus - minus)
        return carry

    lax.fori_loop(0, KBLOCKS, longitudes, 0)
    for j in range(2):
        high, low = tend_ref[2 * j], tend_ref[2 * j + 1]
        back = dot(table3(ana_ref, j, slice(0, M)), jnp.concatenate([high, low, high], axis=0))
        for h in range(QB // 2):
            part = back[:, h * LANES : (h + 1) * LANES]
            out_ref[pl.ds(row * QB + j * (QB // 2) + h, M, stride=step), :] = part


def physics(rows, arrived, tables, gain, weight_in, bias, weight_out):
    total = M * rows * QB
    whole = lambda shape: pl.BlockSpec(shape, lambda r: (0,) * len(shape))
    operands = (arrived, *tables, gain, weight_in, bias, weight_out)
    return pl.pallas_call(
        functools.partial(physics_kernel, rows),
        out_shape=jax.ShapeDtypeStruct((total, LANES), F32),
        grid=(rows,),
        in_specs=[whole(x.shape) for x in operands],
        out_specs=whole((total, LANES)),
        scratch_shapes=[
            pltpu.VMEM((3 * C, HIDDEN), BF16),
            pltpu.VMEM((3 * HIDDEN, C), BF16),
            pltpu.VMEM((4, KPAD, C), BF16),
        ],
        compiler_params=pltpu.CompilerParams(vmem_limit_bytes=63 * MIB),
        cost_estimate=pl.CostEstimate(
            flops=6 * rows * KPAD * (4 * M * C + 4 * C * HIDDEN),
            bytes_accessed=8 * total * LANES + 16 * KPAD * M,
            transcendentals=2 * rows * KPAD * HIDDEN,
        ),
        name="column_physics",
    )(*operands)


def turn_kernel(waves_ref, weight_ref, *refs):
    leg_refs, out_ref, turned = refs[:-2], refs[-2], refs[-1]
    wave = own_wave(waves_ref, pl.program_id(0))
    degrees = lax.broadcasted_iota(jnp.int32, (M, 1), 0)
    keep = jnp.where(degrees >= wave, 1.0, 0.0).astype(F32)
    count = weight_ref.shape[0]
    rows = jnp.concatenate([ref[0] for ref in leg_refs], axis=0) * weight_ref[...]
    if count % LANES:
        rows = jnp.concatenate([rows, jnp.zeros((LANES - count % LANES, M), F32)], axis=0)
    table = rows.T * keep
    for j in range(turned.shape[0]):
        turned[j] = table[:, j * LANES : (j + 1) * LANES]
    for parity in range(2):
        half = [
            turned.at[j][pl.ds(parity, M // 2, stride=2), :] for j in range(turned.shape[0])
        ]
        out_ref[0, parity] = jnp.concatenate(
            split(jnp.concatenate(half, axis=1)[:, :count]), axis=1
        )


def turn(chunk, waves, weights, legendre):
    first, count = span_of(chunk)
    shape = (1, 2, M // 2, 2 * count)
    return pl.pallas_call(
        turn_kernel,
        out_shape=jax.ShapeDtypeStruct((SLOTS,) + shape[1:], BF16),
        grid=(SLOTS,),
        in_specs=[
            pl.BlockSpec(memory_space=pltpu.SMEM),
            pl.BlockSpec((count, 1), lambda s: (0, 0)),
        ]
        + [pl.BlockSpec((1, BLOCK, M), lambda s, k=k: (s, k, 0)) for k in blocks_of(chunk)],
        out_specs=pl.BlockSpec(shape, lambda s: (s, 0, 0, 0)),
        scratch_shapes=[pltpu.VMEM((-(-count // LANES), M, LANES), F32)],
        compiler_params=pltpu.CompilerParams(vmem_limit_bytes=48 * MIB),
        name="turned_tables",
    )(waves, weights[first : first + count], *([legendre] * len(blocks_of(chunk))))


def analyse_kernel(chunk, last, waves_hbm, arrived_hbm, table_hbm, *refs):
    if last:
        partial_hbm, out_hbm, *refs, partial, part_sem = refs
    else:
        out_hbm, *refs = refs
    waves_ref, waves_sem, arrived, table, in_sem, table_sem, out, out_sem = refs
    rows = len(chunk)
    count = span_of(chunk)[1]
    blocks = blocks_of(chunk)

    def fetched(s):
        copies = [
            pltpu.make_async_copy(arrived_hbm.at[:, s], arrived.at[s], in_sem.at[s]),
            pltpu.make_async_copy(table_hbm.at[s], table.at[s], table_sem.at[s]),
        ]
        if last:
            copies.append(pltpu.make_async_copy(partial_hbm.at[s], partial.at[s], part_sem.at[s]))
        return copies

    def sent(s):
        if not last:
            return [pltpu.make_async_copy(out.at[s], out_hbm.at[s], out_sem.at[s, 0])]
        return [
            pltpu.make_async_copy(
                out.at[s, b], out_hbm.at[s, :, b * LANES : (b + 1) * LANES], out_sem.at[s, b]
            )
            for b in range(QB)
        ]

    def work(s):
        wave = own_wave(waves_ref, s)
        flat = arrived.at[s].reshape(DEVICES * rows * QB, LANES)
        values = [
            jnp.concatenate(
                [flat[pl.ds(i * QB + b, DEVICES, stride=rows * QB), :] for b in range(QB)], axis=1
            )
            for i in range(rows)
        ]
        halves = {
            piece: values[i][h * BLOCK : (h + 1) * BLOCK]
            for i, row in enumerate(chunk)
            for h, piece in enumerate(row)
        }
        north = jnp.concatenate([halves[k, False] for k in blocks], axis=0)
        south = jnp.concatenate([halves[k, True] for k in blocks], axis=0)
        for parity in range(2):
            sign = jnp.where((wave + parity) % 2 == 0, 1.0, -1.0).astype(F32)
            high, low = split(north + sign * south)
            left = table.at[s, parity]
            term = dot(left[...], jnp.concatenate([high, high], axis=0))
            term = term + dot(left[:, :count], low)
            if last:
                term = term + partial[s, parity]
                for b in range(QB):
                    out.at[s, b][pl.ds(parity, M // 2, stride=2), :] = (
                        term[:, b * LANES : (b + 1) * LANES]
                    )
            else:
                out[s, parity] = term
        for copy in sent(s):
            copy.start()

    each_slot(pltpu.make_async_copy(waves_hbm, waves_ref, waves_sem), fetched, work)
    for s in range(SLOTS):
        for copy in sent(s):
            copy.wait()


def analyse(chunk, waves, arrived, table, partial=None):
    rows = len(chunk)
    last = partial is not None
    tail = (rows * QB, LANES) if rows * QB % 8 == 0 else (rows, QB, LANES)
    split_shape = (SLOTS, 2, M // 2, 2 * C)
    shape = (SLOTS, M, 2 * C) if last else split_shape
    hbm = pl.BlockSpec(memory_space=pltpu.HBM)
    semaphores = pltpu.SemaphoreType.DMA((SLOTS,))
    return pl.pallas_call(
        functools.partial(analyse_kernel, chunk, last),
        out_shape=jax.ShapeDtypeStruct(shape, F32),
        in_specs=[hbm] * (4 if last else 3),
        out_specs=hbm,
        scratch_shapes=[
            pltpu.SMEM((M,), jnp.int32),
            pltpu.SemaphoreType.DMA,
            pltpu.VMEM((SLOTS, DEVICES) + tail, F32),
            pltpu.VMEM(table.shape, BF16),
            semaphores,
            semaphores,
            pltpu.VMEM((SLOTS, QB, M, LANES) if last else shape, F32),
            pltpu.SemaphoreType.DMA((SLOTS, QB)),
        ]
        + [pltpu.VMEM(split_shape, F32), semaphores] * last,
        compiler_params=pltpu.CompilerParams(vmem_limit_bytes=60 * MIB),
        cost_estimate=pl.CostEstimate(
            flops=3 * SLOTS * DEVICES * rows * M * 2 * C,
            bytes_accessed=4 * (SLOTS * M * 2 * C * 2 + arrived.size),
            transcendentals=0,
        ),
        name="legendre_analysis",
    )(waves, arrived.reshape((DEVICES, SLOTS) + tail), table, *((partial,) if last else ()))


def exchange(value, rows):
    pieces = value.reshape(DEVICES, SLOTS * rows, QB, LANES)
    moved = lax.all_to_all(pieces, AXES, split_axis=0, concat_axis=0, tiled=True)
    return moved.reshape(M * rows * QB, LANES)


def body(spectrum, legendre, wave_table, quad_weight, norm_gain, weight_in, bias_in, weight_out):
    weights = quad_weight[:, None]
    gain, bias = norm_gain[None, :], bias_in[None, :]
    tables = fourier_tables(wave_table)
    turned = [turn(chunk, wave_table, weights, legendre) for chunk in CHUNKS]
    arrived = [
        exchange(synth(chunk, wave_table, spectrum, legendre), len(chunk)) for chunk in CHUNKS
    ]
    back = [
        exchange(
            physics(len(chunk), value, tables, gain, weight_in, bias, weight_out), len(chunk)
        )
        for chunk, value in zip(CHUNKS, arrived)
    ]
    total = None
    for chunk, value, table in zip(CHUNKS, back, turned):
        total = analyse(chunk, wave_table, value, table, total)
    return total


def solution(mesh):
    return jax.shard_map(
        body,
        mesh=mesh,
        in_specs=(P(AXES, None, None), P(AXES, None, None), P(), P(), P(), P(), P(), P()),
        out_specs=P(AXES, None, None),
        check_vma=False,
    )
```

```python
import functools
import math

import jax
import jax.numpy as jnp
from jax import lax
from jax.experimental import pallas as pl
from jax.experimental.pallas import tpu as pltpu
from jax.sharding import PartitionSpec as P

M = 640
C = 256
HALF = 320
NLON = 1280
HIDDEN = 512
DEVICES = 128
SLOTS = M // DEVICES
LANES = 128
QB = 2 * C // LANES
BLOCK = 64
SKIP = 256
KPAD = 672
KBLOCKS = 2
KB = KPAD // KBLOCKS
AHEAD = 3
AXES = ("lat", "lon")
MIB = 1024 * 1024
F32 = jnp.float32
BF16 = jnp.bfloat16

CHUNKS = (
    (((0, False), (1, False)), ((0, True), (1, True))),
    (((2, False), (3, False)), ((2, True), (3, True)), ((4, False), (4, True))),
)


def blocks_of(chunk):
    return sorted({block for row in chunk for block, _ in row})


def span_of(chunk):
    blocks = blocks_of(chunk)
    return blocks[0] * BLOCK, len(blocks) * BLOCK


def own_wave(waves_ref, slot):
    return waves_ref[lax.axis_index(AXES) * SLOTS + slot]


def split(value):
    high = value.astype(BF16)
    low = (value - high.astype(F32)).astype(BF16)
    return high, low


def across3(value):
    high, low = split(value)
    return jnp.concatenate([high, high, low], axis=1)


def down3(value):
    high, low = split(value)
    return jnp.concatenate([high, low, high], axis=0)


def dot(left, right):
    return jnp.dot(left, right, preferred_element_type=F32)


def each_slot(first, waves_ref, copies, low_copies, work):
    def low(s):
        return own_wave(waves_ref, s) < SKIP

    def begin(s):
        for copy in copies(s):
            copy.start()

    def begin_low(s):
        for copy in low_copies(s):
            copy.start()

    def wait_low(s):
        for copy in low_copies(s):
            copy.wait()

    def step(s, carry):
        @pl.when(s + AHEAD < SLOTS)
        def _():
            begin(s + AHEAD)
            pl.when(low(s + AHEAD))(lambda: begin_low(s + AHEAD))

        for copy in copies(s):
            copy.wait()
        pl.when(low(s))(lambda: wait_low(s))
        work(s)
        return carry

    first.start()
    begin(0)
    first.wait()
    pl.when(low(0))(lambda: begin_low(0))
    for s in range(1, AHEAD):
        begin(s)
        pl.when(low(s))(functools.partial(begin_low, s))
    lax.fori_loop(0, SLOTS, step, 0)


def synth_kernel(
    chunk,
    waves_hbm,
    spec_hbm,
    leg_hbm,
    out_hbm,
    waves_ref,
    waves_sem,
    spec,
    leg,
    out,
    spec_sem,
    leg_sem,
    out_sem,
    low_sem,
):
    rows = len(chunk)
    first, count = span_of(chunk)
    blocks = blocks_of(chunk)
    by_slot = out.ndim > 2
    across = lax.broadcasted_iota(jnp.int32, (1, M), 1)

    def fetched(s):
        return (
            pltpu.make_async_copy(
                leg_hbm.at[s, pl.ds(first, count), :], leg.at[s], leg_sem.at[s]
            ),
            pltpu.make_async_copy(
                spec_hbm.at[s, pl.ds(SKIP, M - SKIP), :],
                spec.at[s, pl.ds(SKIP, M - SKIP), :],
                spec_sem.at[s],
            ),
        )

    def fetched_low(s):
        return (
            pltpu.make_async_copy(
                spec_hbm.at[s, pl.ds(0, SKIP), :], spec.at[s, pl.ds(0, SKIP), :], low_sem.at[s]
            ),
        )

    def sent(s):
        if by_slot:
            return pltpu.make_async_copy(out.at[s], out_hbm.at[:, s], out_sem.at[s])
        return pltpu.make_async_copy(out, out_hbm, out_sem.at[0])

    def work(s):
        wave = own_wave(waves_ref, s)
        pl.when(wave < SKIP)(lambda: multiply(s, wave, 0))
        pl.when(wave >= SKIP)(lambda: multiply(s, wave, SKIP))
        if by_slot:
            sent(s).start()

    def multiply(s, wave, least):
        degrees = across[:, least:]
        keep = jnp.where(degrees >= wave, 1.0, 0.0).astype(F32)
        sign = jnp.where((degrees + wave) % 2 == 0, 1.0, -1.0).astype(BF16)
        sign = jnp.concatenate([sign] * 3, axis=1)
        parts = {}
        for j, block in enumerate(blocks):
            table = across3(leg[s, j * BLOCK : (j + 1) * BLOCK, least:] * keep)
            parts[block, False] = table
            parts[block, True] = table * sign
        left = jnp.concatenate([parts[piece] for row in chunk for piece in row], axis=0)
        fourier = dot(left, down3(spec[s, least:]))
        if by_slot:
            flat, begin, stride = out.at[s].reshape(DEVICES * rows * QB, LANES), 0, rows * QB
        else:
            flat, begin, stride = out, s * rows * QB, SLOTS * rows * QB
        for i in range(rows):
            for b in range(QB):
                part = fourier[i * DEVICES : (i + 1) * DEVICES, b * LANES : (b + 1) * LANES]
                if b >= QB // 2:
                    part = jnp.where(wave > 0, part, 0.0)
                flat[pl.ds(begin + i * QB + b, DEVICES, stride=stride), :] = part

    waves_copy = pltpu.make_async_copy(waves_hbm, waves_ref, waves_sem)
    each_slot(waves_copy, waves_ref, fetched, fetched_low, work)
    if not by_slot:
        sent(0).start()
    for s in range(SLOTS if by_slot else 1):
        sent(s).wait()


def synth(chunk, waves, spectrum, legendre):
    rows = len(chunk)
    count = span_of(chunk)[1]
    if rows * QB % 8 == 0:
        shape = (DEVICES, SLOTS, rows * QB, LANES)
        buffer = (SLOTS, DEVICES, rows * QB, LANES)
    else:
        shape = buffer = (DEVICES * SLOTS * rows * QB, LANES)
    hbm = pl.BlockSpec(memory_space=pltpu.HBM)
    return pl.pallas_call(
        functools.partial(synth_kernel, chunk),
        out_shape=jax.ShapeDtypeStruct(shape, F32),
        in_specs=[hbm, hbm, hbm],
        out_specs=hbm,
        scratch_shapes=[
            pltpu.SMEM((M,), jnp.int32),
            pltpu.SemaphoreType.DMA,
            pltpu.VMEM((SLOTS, M, 2 * C), F32),
            pltpu.VMEM((SLOTS, count, M), F32),
            pltpu.VMEM(buffer, F32),
        ]
        + [pltpu.SemaphoreType.DMA((SLOTS,))] * 4,
        compiler_params=pltpu.CompilerParams(vmem_limit_bytes=63 * MIB),
        cost_estimate=pl.CostEstimate(
            flops=6 * SLOTS * DEVICES * rows * M * 2 * C,
            bytes_accessed=4 * SLOTS * (2 * M * C + count * M + DEVICES * rows * 2 * C),
            transcendentals=0,
        ),
        name="legendre_synthesis",
    )(waves, spectrum, legendre)


def tables_kernel(waves_ref, cos_ref, sin_ref, syn_ref, ana_ref):
    amplitude = jnp.where(waves_ref[...] == 0, 1.0, 2.0).astype(F32)
    longitudes = lax.broadcasted_iota(jnp.int32, (1, KPAD), 1)
    edge = (longitudes == 0) | (longitudes == NLON // 2)
    share = jnp.where(longitudes > NLON // 2, 0.0, jnp.where(edge, 0.5, 1.0) / NLON).astype(F32)
    for j, ref in enumerate((cos_ref, sin_ref)):
        table = ref[...]
        syn_ref[2 * j], syn_ref[2 * j + 1] = split(table.T * amplitude)
        ana_ref[2 * j], ana_ref[2 * j + 1] = split(table * (share if j == 0 else -share))


def fourier_tables(wave_table):
    longitudes = jnp.arange(KPAD, dtype=jnp.int32)
    angles = (wave_table[:, None] * longitudes[None, :] % NLON).astype(F32) * (2.0 * math.pi / NLON)
    return pl.pallas_call(
        tables_kernel,
        out_shape=(
            jax.ShapeDtypeStruct((4, KPAD, M), BF16),
            jax.ShapeDtypeStruct((4, M, KPAD), BF16),
        ),
        compiler_params=pltpu.CompilerParams(vmem_limit_bytes=48 * MIB),
        name="fourier_tables",
    )(wave_table[None, :], jnp.cos(angles), jnp.sin(angles))


def physics_kernel(
    rows,
    x_ref,
    syn_ref,
    ana_ref,
    gain_ref,
    win_ref,
    bias_ref,
    wout_ref,
    out_ref,
    w1_ref,
    w2_ref,
    tend_ref,
):
    row = pl.program_id(0)

    @pl.when(row == 0)
    def _():
        w1_ref[...] = down3(win_ref[...])
        w2_ref[...] = down3(wout_ref[...])

    step = rows * QB
    parts = [x_ref[pl.ds(row * QB + b, M, stride=step), :] for b in range(QB)]
    real = down3(jnp.concatenate(parts[: QB // 2], axis=1))
    imag = down3(jnp.concatenate(parts[QB // 2 :], axis=1))

    def table3(ref, j, rng):
        high, low = ref[2 * j, rng, :], ref[2 * j + 1, rng, :]
        return jnp.concatenate([high, high, low], axis=1)

    def longitudes(k, carry):
        rng = pl.ds(pl.multiple_of(k * KB, KB), KB)
        even = dot(table3(syn_ref, 0, rng), real)
        odd = dot(table3(syn_ref, 1, rng), imag)
        columns = jnp.concatenate([even - odd, even + odd], axis=0)
        mean_square = jnp.mean(columns * columns, axis=-1, keepdims=True)
        normed = columns * gain_ref[...] * lax.rsqrt(mean_square + 1e-06)
        hidden = dot(across3(normed), w1_ref[...]) + bias_ref[...]
        hidden = hidden / (1.0 + jnp.exp(-hidden))
        tendency = dot(across3(hidden), w2_ref[...])
        plus, minus = tendency[:KB], tendency[KB:]
        tend_ref[0, rng, :], tend_ref[1, rng, :] = split(plus + minus)
        tend_ref[2, rng, :], tend_ref[3, rng, :] = split(plus - minus)
        return carry

    lax.fori_loop(0, KBLOCKS, longitudes, 0)
    for j in range(2):
        high, low = tend_ref[2 * j], tend_ref[2 * j + 1]
        back = dot(table3(ana_ref, j, slice(0, M)), jnp.concatenate([high, low, high], axis=0))
        for h in range(QB // 2):
            part = back[:, h * LANES : (h + 1) * LANES]
            out_ref[pl.ds(row * QB + j * (QB // 2) + h, M, stride=step), :] = part


def physics(rows, arrived, tables, gain, weight_in, bias, weight_out):
    total = M * rows * QB
    whole = lambda shape: pl.BlockSpec(shape, lambda r: (0,) * len(shape))
    operands = (arrived, *tables, gain, weight_in, bias, weight_out)
    return pl.pallas_call(
        functools.partial(physics_kernel, rows),
        out_shape=jax.ShapeDtypeStruct((total, LANES), F32),
        grid=(rows,),
        in_specs=[whole(x.shape) for x in operands],
        out_specs=whole((total, LANES)),
        scratch_shapes=[
            pltpu.VMEM((3 * C, HIDDEN), BF16),
            pltpu.VMEM((3 * HIDDEN, C), BF16),
            pltpu.VMEM((4, KPAD, C), BF16),
        ],
        compiler_params=pltpu.CompilerParams(vmem_limit_bytes=63 * MIB),
        cost_estimate=pl.CostEstimate(
            flops=6 * rows * KPAD * (4 * M * C + 4 * C * HIDDEN),
            bytes_accessed=8 * total * LANES + 16 * KPAD * M,
            transcendentals=2 * rows * KPAD * HIDDEN,
        ),
        name="column_physics",
    )(*operands)


def turn_kernel(waves_ref, weight_ref, *refs):
    leg_refs, out_ref, turned = refs[:-2], refs[-2], refs[-1]
    wave = own_wave(waves_ref, pl.program_id(0))
    degrees = lax.broadcasted_iota(jnp.int32, (M, 1), 0)
    keep = jnp.where(degrees >= wave, 1.0, 0.0).astype(F32)
    count = weight_ref.shape[0]
    rows = jnp.concatenate([ref[0] for ref in leg_refs], axis=0) * weight_ref[...]
    if count % LANES:
        rows = jnp.concatenate([rows, jnp.zeros((LANES - count % LANES, M), F32)], axis=0)
    table = rows.T * keep
    for j in range(turned.shape[0]):
        turned[j] = table[:, j * LANES : (j + 1) * LANES]
    for parity in range(2):
        half = [
            turned.at[j][pl.ds(parity, M // 2, stride=2), :] for j in range(turned.shape[0])
        ]
        out_ref[0, parity] = jnp.concatenate(
            split(jnp.concatenate(half, axis=1)[:, :count]), axis=1
        )


def turn(chunk, waves, weights, legendre):
    first, count = span_of(chunk)
    shape = (1, 2, M // 2, 2 * count)
    return pl.pallas_call(
        turn_kernel,
        out_shape=jax.ShapeDtypeStruct((SLOTS,) + shape[1:], BF16),
        grid=(SLOTS,),
        in_specs=[
            pl.BlockSpec(memory_space=pltpu.SMEM),
            pl.BlockSpec((count, 1), lambda s: (0, 0)),
        ]
        + [pl.BlockSpec((1, BLOCK, M), lambda s, k=k: (s, k, 0)) for k in blocks_of(chunk)],
        out_specs=pl.BlockSpec(shape, lambda s: (s, 0, 0, 0)),
        scratch_shapes=[pltpu.VMEM((-(-count // LANES), M, LANES), F32)],
        compiler_params=pltpu.CompilerParams(vmem_limit_bytes=48 * MIB),
        name="turned_tables",
    )(waves, weights[first : first + count], *([legendre] * len(blocks_of(chunk))))


def analyse_kernel(chunk, last, waves_hbm, arrived_hbm, table_hbm, *refs):
    if last:
        partial_hbm, out_hbm, *refs, partial, part_sem, low_sem = refs
    else:
        out_hbm, *refs = refs
    waves_ref, waves_sem, arrived, table, in_sem, table_sem, out, out_sem = refs
    rows = len(chunk)
    count = span_of(chunk)[1]
    blocks = blocks_of(chunk)

    skipped = SKIP // 2 if last else 0
    high = pl.ds(skipped, M // 2 - skipped)
    low = pl.ds(0, skipped)

    def fetched(s):
        copies = [
            pltpu.make_async_copy(arrived_hbm.at[:, s], arrived.at[s], in_sem.at[s]),
            pltpu.make_async_copy(
                table_hbm.at[s, :, high], table.at[s, :, high], table_sem.at[s]
            ),
        ]
        if last:
            copies.append(
                pltpu.make_async_copy(
                    partial_hbm.at[s, :, high], partial.at[s, :, high], part_sem.at[s]
                )
            )
        return copies

    def fetched_low(s):
        if not last:
            return []
        return [
            pltpu.make_async_copy(
                table_hbm.at[s, :, low], table.at[s, :, low], low_sem.at[s, 0]
            ),
            pltpu.make_async_copy(
                partial_hbm.at[s, :, low], partial.at[s, :, low], low_sem.at[s, 1]
            ),
        ]

    def sent(s):
        if not last:
            return [pltpu.make_async_copy(out.at[s], out_hbm.at[s], out_sem.at[s, 0])]
        return [
            pltpu.make_async_copy(
                out.at[s, b], out_hbm.at[s, :, b * LANES : (b + 1) * LANES], out_sem.at[s, b]
            )
            for b in range(QB)
        ]

    def work(s):
        wave = own_wave(waves_ref, s)
        flat = arrived.at[s].reshape(DEVICES * rows * QB, LANES)
        values = [
            jnp.concatenate(
                [flat[pl.ds(i * QB + b, DEVICES, stride=rows * QB), :] for b in range(QB)], axis=1
            )
            for i in range(rows)
        ]
        halves = {
            piece: values[i][h * BLOCK : (h + 1) * BLOCK]
            for i, row in enumerate(chunk)
            for h, piece in enumerate(row)
        }
        north = jnp.concatenate([halves[k, False] for k in blocks], axis=0)
        south = jnp.concatenate([halves[k, True] for k in blocks], axis=0)
        right = []
        for parity in range(2):
            sign = jnp.where((wave + parity) % 2 == 0, 1.0, -1.0).astype(F32)
            right.append(split(north + sign * south))
        if last:
            pl.when(wave < SKIP)(lambda: multiply(s, right, 0))
            pl.when(wave >= SKIP)(lambda: multiply(s, right, skipped))
        else:
            multiply(s, right, 0)
        for copy in sent(s):
            copy.start()

    def multiply(s, right, least):
        for parity in range(2):
            top, rest = right[parity]
            left = table.at[s, parity]
            term = dot(left[least:, :], jnp.concatenate([top, top], axis=0))
            term = term + dot(left[least:, :count], rest)
            if not last:
                out[s, parity] = term
                continue
            term = term + partial[s, parity, least:, :]
            for b in range(QB):
                target = out.at[s, b]
                part = term[:, b * LANES : (b + 1) * LANES]
                target[pl.ds(2 * least + parity, M // 2 - least, stride=2), :] = part
        if least:
            for b in range(QB):
                out[s, b, : 2 * least, :] = jnp.zeros((2 * least, LANES), F32)

    waves_copy = pltpu.make_async_copy(waves_hbm, waves_ref, waves_sem)
    each_slot(waves_copy, waves_ref, fetched, fetched_low, work)
    for s in range(SLOTS):
        for copy in sent(s):
            copy.wait()


def analyse(chunk, waves, arrived, table, partial=None):
    rows = len(chunk)
    last = partial is not None
    tail = (rows * QB, LANES) if rows * QB % 8 == 0 else (rows, QB, LANES)
    split_shape = (SLOTS, 2, M // 2, 2 * C)
    shape = (SLOTS, M, 2 * C) if last else split_shape
    hbm = pl.BlockSpec(memory_space=pltpu.HBM)
    semaphores = pltpu.SemaphoreType.DMA((SLOTS,))
    return pl.pallas_call(
        functools.partial(analyse_kernel, chunk, last),
        out_shape=jax.ShapeDtypeStruct(shape, F32),
        in_specs=[hbm] * (4 if last else 3),
        out_specs=hbm,
        scratch_shapes=[
            pltpu.SMEM((M,), jnp.int32),
            pltpu.SemaphoreType.DMA,
            pltpu.VMEM((SLOTS, DEVICES) + tail, F32),
            pltpu.VMEM(table.shape, BF16),
            semaphores,
            semaphores,
            pltpu.VMEM((SLOTS, QB, M, LANES) if last else shape, F32),
            pltpu.SemaphoreType.DMA((SLOTS, QB)),
        ]
        + [pltpu.VMEM(split_shape, F32), semaphores, pltpu.SemaphoreType.DMA((SLOTS, 2))] * last,
        compiler_params=pltpu.CompilerParams(vmem_limit_bytes=60 * MIB),
        cost_estimate=pl.CostEstimate(
            flops=3 * SLOTS * DEVICES * rows * M * 2 * C,
            bytes_accessed=4 * (SLOTS * M * 2 * C * 2 + arrived.size),
            transcendentals=0,
        ),
        name="legendre_analysis",
    )(waves, arrived.reshape((DEVICES, SLOTS) + tail), table, *((partial,) if last else ()))


def exchange(value, rows):
    pieces = value.reshape(DEVICES, SLOTS * rows, QB, LANES)
    moved = lax.all_to_all(pieces, AXES, split_axis=0, concat_axis=0, tiled=True)
    return moved.reshape(M * rows * QB, LANES)


def body(spectrum, legendre, wave_table, quad_weight, norm_gain, weight_in, bias_in, weight_out):
    weights = quad_weight[:, None]
    gain, bias = norm_gain[None, :], bias_in[None, :]
    tables = fourier_tables(wave_table)
    turned = [turn(chunk, wave_table, weights, legendre) for chunk in CHUNKS]
    arrived = [
        exchange(synth(chunk, wave_table, spectrum, legendre), len(chunk)) for chunk in CHUNKS
    ]
    back = [
        exchange(
            physics(len(chunk), value, tables, gain, weight_in, bias, weight_out), len(chunk)
        )
        for chunk, value in zip(CHUNKS, arrived)
    ]
    total = None
    for chunk, value, table in zip(CHUNKS, back, turned):
        total = analyse(chunk, wave_table, value, table, total)
    return total


def solution(mesh):
    return jax.shard_map(
        body,
        mesh=mesh,
        in_specs=(P(AXES, None, None), P(AXES, None, None), P(), P(), P(), P(), P(), P()),
        out_specs=P(AXES, None, None),
        check_vma=False,
    )
```

```python
import functools
import math

import jax
import jax.numpy as jnp
from jax import lax
from jax.experimental import pallas as pl
from jax.experimental.pallas import tpu as pltpu
from jax.sharding import PartitionSpec as P

M = 640
C = 256
HALF = 320
NLON = 1280
HIDDEN = 512
DEVICES = 128
SLOTS = M // DEVICES
LANES = 128
QB = 2 * C // LANES
BLOCK = 64
SKIP = 128
KPAD = 672
KBLOCKS = 2
KB = KPAD // KBLOCKS
AHEAD = 3
AXES = ("lat", "lon")
MIB = 1024 * 1024
F32 = jnp.float32
BF16 = jnp.bfloat16

CHUNKS = (
    (((0, False), (1, False)), ((0, True), (1, True))),
    (((2, False), (3, False)), ((2, True), (3, True)), ((4, False), (4, True))),
)


def blocks_of(chunk):
    return sorted({block for row in chunk for block, _ in row})


def span_of(chunk):
    blocks = blocks_of(chunk)
    return blocks[0] * BLOCK, len(blocks) * BLOCK


def own_wave(waves_ref, slot):
    return waves_ref[lax.axis_index(AXES) * SLOTS + slot]


def split(value):
    high = value.astype(BF16)
    low = (value - high.astype(F32)).astype(BF16)
    return high, low


def across3(value):
    high, low = split(value)
    return jnp.concatenate([high, high, low], axis=1)


def down3(value):
    high, low = split(value)
    return jnp.concatenate([high, low, high], axis=0)


def dot(left, right):
    return jnp.dot(left, right, preferred_element_type=F32)


def each_slot(first, waves_ref, copies, low_copies, work):
    def low(s):
        return own_wave(waves_ref, s) < SKIP

    def begin(s):
        for copy in copies(s):
            copy.start()

    def begin_low(s):
        for copy in low_copies(s):
            copy.start()

    def wait_low(s):
        for copy in low_copies(s):
            copy.wait()

    def step(s, carry):
        @pl.when(s + AHEAD < SLOTS)
        def _():
            begin(s + AHEAD)
            pl.when(low(s + AHEAD))(lambda: begin_low(s + AHEAD))

        for copy in copies(s):
            copy.wait()
        pl.when(low(s))(lambda: wait_low(s))
        work(s)
        return carry

    first.start()
    begin(0)
    first.wait()
    pl.when(low(0))(lambda: begin_low(0))
    for s in range(1, AHEAD):
        begin(s)
        pl.when(low(s))(functools.partial(begin_low, s))
    lax.fori_loop(0, SLOTS, step, 0)


def synth_kernel(
    chunk,
    waves_hbm,
    spec_hbm,
    leg_hbm,
    out_hbm,
    waves_ref,
    waves_sem,
    spec,
    leg,
    out,
    spec_sem,
    leg_sem,
    out_sem,
    low_sem,
):
    rows = len(chunk)
    first, count = span_of(chunk)
    blocks = blocks_of(chunk)
    by_slot = out.ndim > 2
    across = lax.broadcasted_iota(jnp.int32, (1, M), 1)

    def fetched(s):
        return (
            pltpu.make_async_copy(
                leg_hbm.at[s, pl.ds(first, count), :], leg.at[s], leg_sem.at[s]
            ),
            pltpu.make_async_copy(
                spec_hbm.at[s, pl.ds(SKIP, M - SKIP), :],
                spec.at[s, pl.ds(SKIP, M - SKIP), :],
                spec_sem.at[s],
            ),
        )

    def fetched_low(s):
        return (
            pltpu.make_async_copy(
                spec_hbm.at[s, pl.ds(0, SKIP), :], spec.at[s, pl.ds(0, SKIP), :], low_sem.at[s]
            ),
        )

    def sent(s):
        if by_slot:
            return pltpu.make_async_copy(out.at[s], out_hbm.at[:, s], out_sem.at[s])
        return pltpu.make_async_copy(out, out_hbm, out_sem.at[0])

    def work(s):
        wave = own_wave(waves_ref, s)
        pl.when(wave < SKIP)(lambda: multiply(s, wave, 0))
        pl.when(wave >= SKIP)(lambda: multiply(s, wave, SKIP))
        if by_slot:
            sent(s).start()

    def multiply(s, wave, least):
        degrees = across[:, least:]
        keep = jnp.where(degrees >= wave, 1.0, 0.0).astype(F32)
        sign = jnp.where((degrees + wave) % 2 == 0, 1.0, -1.0).astype(BF16)
        sign = jnp.concatenate([sign] * 3, axis=1)
        parts = {}
        for j, block in enumerate(blocks):
            table = across3(leg[s, j * BLOCK : (j + 1) * BLOCK, least:] * keep)
            parts[block, False] = table
            parts[block, True] = table * sign
        left = jnp.concatenate([parts[piece] for row in chunk for piece in row], axis=0)
        fourier = dot(left, down3(spec[s, least:]))
        if by_slot:
            flat, begin, stride = out.at[s].reshape(DEVICES * rows * QB, LANES), 0, rows * QB
        else:
            flat, begin, stride = out, s * rows * QB, SLOTS * rows * QB
        for i in range(rows):
            for b in range(QB):
                part = fourier[i * DEVICES : (i + 1) * DEVICES, b * LANES : (b + 1) * LANES]
                if b >= QB // 2:
                    part = jnp.where(wave > 0, part, 0.0)
                flat[pl.ds(begin + i * QB + b, DEVICES, stride=stride), :] = part

    waves_copy = pltpu.make_async_copy(waves_hbm, waves_ref, waves_sem)
    each_slot(waves_copy, waves_ref, fetched, fetched_low, work)
    if not by_slot:
        sent(0).start()
    for s in range(SLOTS if by_slot else 1):
        sent(s).wait()


def synth(chunk, waves, spectrum, legendre):
    rows = len(chunk)
    count = span_of(chunk)[1]
    if rows * QB % 8 == 0:
        shape = (DEVICES, SLOTS, rows * QB, LANES)
        buffer = (SLOTS, DEVICES, rows * QB, LANES)
    else:
        shape = buffer = (DEVICES * SLOTS * rows * QB, LANES)
    hbm = pl.BlockSpec(memory_space=pltpu.HBM)
    return pl.pallas_call(
        functools.partial(synth_kernel, chunk),
        out_shape=jax.ShapeDtypeStruct(shape, F32),
        in_specs=[hbm, hbm, hbm],
        out_specs=hbm,
        scratch_shapes=[
            pltpu.SMEM((M,), jnp.int32),
            pltpu.SemaphoreType.DMA,
            pltpu.VMEM((SLOTS, M, 2 * C), F32),
            pltpu.VMEM((SLOTS, count, M), F32),
            pltpu.VMEM(buffer, F32),
        ]
        + [pltpu.SemaphoreType.DMA((SLOTS,))] * 4,
        compiler_params=pltpu.CompilerParams(vmem_limit_bytes=63 * MIB),
        cost_estimate=pl.CostEstimate(
            flops=6 * SLOTS * DEVICES * rows * M * 2 * C,
            bytes_accessed=4 * SLOTS * (2 * M * C + count * M + DEVICES * rows * 2 * C),
            transcendentals=0,
        ),
        name="legendre_synthesis",
    )(waves, spectrum, legendre)


def tables_kernel(waves_ref, cos_ref, sin_ref, syn_ref, ana_ref):
    amplitude = jnp.where(waves_ref[...] == 0, 1.0, 2.0).astype(F32)
    longitudes = lax.broadcasted_iota(jnp.int32, (1, KPAD), 1)
    edge = (longitudes == 0) | (longitudes == NLON // 2)
    share = jnp.where(longitudes > NLON // 2, 0.0, jnp.where(edge, 0.5, 1.0) / NLON).astype(F32)
    for j, ref in enumerate((cos_ref, sin_ref)):
        table = ref[...]
        syn_ref[2 * j], syn_ref[2 * j + 1] = split(table.T * amplitude)
        ana_ref[2 * j], ana_ref[2 * j + 1] = split(table * (share if j == 0 else -share))


def fourier_tables(wave_table):
    longitudes = jnp.arange(KPAD, dtype=jnp.int32)
    angles = (wave_table[:, None] * longitudes[None, :] % NLON).astype(F32) * (2.0 * math.pi / NLON)
    return pl.pallas_call(
        tables_kernel,
        out_shape=(
            jax.ShapeDtypeStruct((4, KPAD, M), BF16),
            jax.ShapeDtypeStruct((4, M, KPAD), BF16),
        ),
        compiler_params=pltpu.CompilerParams(vmem_limit_bytes=48 * MIB),
        name="fourier_tables",
    )(wave_table[None, :], jnp.cos(angles), jnp.sin(angles))


def physics_kernel(
    rows,
    x_ref,
    syn_ref,
    ana_ref,
    gain_ref,
    win_ref,
    bias_ref,
    wout_ref,
    out_ref,
    w1_ref,
    w2_ref,
    tend_ref,
):
    row = pl.program_id(0)

    @pl.when(row == 0)
    def _():
        w1_ref[...] = down3(win_ref[...])
        w2_ref[...] = down3(wout_ref[...])

    step = rows * QB
    parts = [x_ref[pl.ds(row * QB + b, M, stride=step), :] for b in range(QB)]
    real = down3(jnp.concatenate(parts[: QB // 2], axis=1))
    imag = down3(jnp.concatenate(parts[QB // 2 :], axis=1))

    def table3(ref, j, rng):
        high, low = ref[2 * j, rng, :], ref[2 * j + 1, rng, :]
        return jnp.concatenate([high, high, low], axis=1)

    def longitudes(k, carry):
        rng = pl.ds(pl.multiple_of(k * KB, KB), KB)
        even = dot(table3(syn_ref, 0, rng), real)
        odd = dot(table3(syn_ref, 1, rng), imag)
        columns = jnp.concatenate([even - odd, even + odd], axis=0)
        mean_square = jnp.mean(columns * columns, axis=-1, keepdims=True)
        normed = columns * gain_ref[...] * lax.rsqrt(mean_square + 1e-06)
        hidden = dot(across3(normed), w1_ref[...]) + bias_ref[...]
        hidden = hidden / (1.0 + jnp.exp(-hidden))
        tendency = dot(across3(hidden), w2_ref[...])
        plus, minus = tendency[:KB], tendency[KB:]
        tend_ref[0, rng, :], tend_ref[1, rng, :] = split(plus + minus)
        tend_ref[2, rng, :], tend_ref[3, rng, :] = split(plus - minus)
        return carry

    lax.fori_loop(0, KBLOCKS, longitudes, 0)
    for j in range(2):
        high, low = tend_ref[2 * j], tend_ref[2 * j + 1]
        back = dot(table3(ana_ref, j, slice(0, M)), jnp.concatenate([high, low, high], axis=0))
        for h in range(QB // 2):
            part = back[:, h * LANES : (h + 1) * LANES]
            out_ref[pl.ds(row * QB + j * (QB // 2) + h, M, stride=step), :] = part


def physics(rows, arrived, tables, gain, weight_in, bias, weight_out):
    total = M * rows * QB
    whole = lambda shape: pl.BlockSpec(shape, lambda r: (0,) * len(shape))
    operands = (arrived, *tables, gain, weight_in, bias, weight_out)
    return pl.pallas_call(
        functools.partial(physics_kernel, rows),
        out_shape=jax.ShapeDtypeStruct((total, LANES), F32),
        grid=(rows,),
        in_specs=[whole(x.shape) for x in operands],
        out_specs=whole((total, LANES)),
        scratch_shapes=[
            pltpu.VMEM((3 * C, HIDDEN), BF16),
            pltpu.VMEM((3 * HIDDEN, C), BF16),
            pltpu.VMEM((4, KPAD, C), BF16),
        ],
        compiler_params=pltpu.CompilerParams(vmem_limit_bytes=63 * MIB),
        cost_estimate=pl.CostEstimate(
            flops=6 * rows * KPAD * (4 * M * C + 4 * C * HIDDEN),
            bytes_accessed=8 * total * LANES + 16 * KPAD * M,
            transcendentals=2 * rows * KPAD * HIDDEN,
        ),
        name="column_physics",
    )(*operands)


def turn_kernel(waves_ref, weight_ref, *refs):
    leg_refs, out_ref, turned = refs[:-2], refs[-2], refs[-1]
    wave = own_wave(waves_ref, pl.program_id(0))
    degrees = lax.broadcasted_iota(jnp.int32, (M, 1), 0)
    keep = jnp.where(degrees >= wave, 1.0, 0.0).astype(F32)
    count = weight_ref.shape[0]
    rows = jnp.concatenate([ref[0] for ref in leg_refs], axis=0) * weight_ref[...]
    if count % LANES:
        rows = jnp.concatenate([rows, jnp.zeros((LANES - count % LANES, M), F32)], axis=0)
    table = rows.T * keep
    for j in range(turned.shape[0]):
        turned[j] = table[:, j * LANES : (j + 1) * LANES]
    for parity in range(2):
        half = [
            turned.at[j][pl.ds(parity, M // 2, stride=2), :] for j in range(turned.shape[0])
        ]
        out_ref[0, parity] = jnp.concatenate(
            split(jnp.concatenate(half, axis=1)[:, :count]), axis=1
        )


def turn(chunk, waves, weights, legendre):
    first, count = span_of(chunk)
    shape = (1, 2, M // 2, 2 * count)
    return pl.pallas_call(
        turn_kernel,
        out_shape=jax.ShapeDtypeStruct((SLOTS,) + shape[1:], BF16),
        grid=(SLOTS,),
        in_specs=[
            pl.BlockSpec(memory_space=pltpu.SMEM),
            pl.BlockSpec((count, 1), lambda s: (0, 0)),
        ]
        + [pl.BlockSpec((1, BLOCK, M), lambda s, k=k: (s, k, 0)) for k in blocks_of(chunk)],
        out_specs=pl.BlockSpec(shape, lambda s: (s, 0, 0, 0)),
        scratch_shapes=[pltpu.VMEM((-(-count // LANES), M, LANES), F32)],
        compiler_params=pltpu.CompilerParams(vmem_limit_bytes=48 * MIB),
        name="turned_tables",
    )(waves, weights[first : first + count], *([legendre] * len(blocks_of(chunk))))


def analyse_kernel(chunk, last, waves_hbm, arrived_hbm, table_hbm, *refs):
    if last:
        partial_hbm, out_hbm, *refs, partial, part_sem, low_sem = refs
    else:
        out_hbm, *refs = refs
    waves_ref, waves_sem, arrived, table, in_sem, table_sem, out, out_sem = refs
    rows = len(chunk)
    count = span_of(chunk)[1]
    blocks = blocks_of(chunk)

    skipped = SKIP // 2 if last else 0
    high = pl.ds(skipped, M // 2 - skipped)
    low = pl.ds(0, skipped)

    def fetched(s):
        copies = [
            pltpu.make_async_copy(arrived_hbm.at[:, s], arrived.at[s], in_sem.at[s]),
            pltpu.make_async_copy(
                table_hbm.at[s, :, high], table.at[s, :, high], table_sem.at[s]
            ),
        ]
        if last:
            copies.append(
                pltpu.make_async_copy(
                    partial_hbm.at[s, :, high], partial.at[s, :, high], part_sem.at[s]
                )
            )
        return copies

    def fetched_low(s):
        if not last:
            return []
        return [
            pltpu.make_async_copy(
                table_hbm.at[s, :, low], table.at[s, :, low], low_sem.at[s, 0]
            ),
            pltpu.make_async_copy(
                partial_hbm.at[s, :, low], partial.at[s, :, low], low_sem.at[s, 1]
            ),
        ]

    def sent(s):
        if not last:
            return [pltpu.make_async_copy(out.at[s], out_hbm.at[s], out_sem.at[s, 0])]
        return [
            pltpu.make_async_copy(
                out.at[s, b], out_hbm.at[s, :, b * LANES : (b + 1) * LANES], out_sem.at[s, b]
            )
            for b in range(QB)
        ]

    def work(s):
        wave = own_wave(waves_ref, s)
        flat = arrived.at[s].reshape(DEVICES * rows * QB, LANES)
        values = [
            jnp.concatenate(
                [flat[pl.ds(i * QB + b, DEVICES, stride=rows * QB), :] for b in range(QB)], axis=1
            )
            for i in range(rows)
        ]
        halves = {
            piece: values[i][h * BLOCK : (h + 1) * BLOCK]
            for i, row in enumerate(chunk)
            for h, piece in enumerate(row)
        }
        north = jnp.concatenate([halves[k, False] for k in blocks], axis=0)
        south = jnp.concatenate([halves[k, True] for k in blocks], axis=0)
        right = []
        for parity in range(2):
            sign = jnp.where((wave + parity) % 2 == 0, 1.0, -1.0).astype(F32)
            right.append(split(north + sign * south))
        if last:
            pl.when(wave < SKIP)(lambda: multiply(s, right, 0))
            pl.when(wave >= SKIP)(lambda: multiply(s, right, skipped))
        else:
            multiply(s, right, 0)
        for copy in sent(s):
            copy.start()

    def multiply(s, right, least):
        for parity in range(2):
            top, rest = right[parity]
            left = table.at[s, parity]
            term = dot(left[least:, :], jnp.concatenate([top, top], axis=0))
            term = term + dot(left[least:, :count], rest)
            if not last:
                out[s, parity] = term
                continue
            term = term + partial[s, parity, least:, :]
            for b in range(QB):
                target = out.at[s, b]
                part = term[:, b * LANES : (b + 1) * LANES]
                target[pl.ds(2 * least + parity, M // 2 - least, stride=2), :] = part
        if least:
            for b in range(QB):
                out[s, b, : 2 * least, :] = jnp.zeros((2 * least, LANES), F32)

    waves_copy = pltpu.make_async_copy(waves_hbm, waves_ref, waves_sem)
    each_slot(waves_copy, waves_ref, fetched, fetched_low, work)
    for s in range(SLOTS):
        for copy in sent(s):
            copy.wait()


def analyse(chunk, waves, arrived, table, partial=None):
    rows = len(chunk)
    last = partial is not None
    tail = (rows * QB, LANES) if rows * QB % 8 == 0 else (rows, QB, LANES)
    split_shape = (SLOTS, 2, M // 2, 2 * C)
    shape = (SLOTS, M, 2 * C) if last else split_shape
    hbm = pl.BlockSpec(memory_space=pltpu.HBM)
    semaphores = pltpu.SemaphoreType.DMA((SLOTS,))
    return pl.pallas_call(
        functools.partial(analyse_kernel, chunk, last),
        out_shape=jax.ShapeDtypeStruct(shape, F32),
        in_specs=[hbm] * (4 if last else 3),
        out_specs=hbm,
        scratch_shapes=[
            pltpu.SMEM((M,), jnp.int32),
            pltpu.SemaphoreType.DMA,
            pltpu.VMEM((SLOTS, DEVICES) + tail, F32),
            pltpu.VMEM(table.shape, BF16),
            semaphores,
            semaphores,
            pltpu.VMEM((SLOTS, QB, M, LANES) if last else shape, F32),
            pltpu.SemaphoreType.DMA((SLOTS, QB)),
        ]
        + [pltpu.VMEM(split_shape, F32), semaphores, pltpu.SemaphoreType.DMA((SLOTS, 2))] * last,
        compiler_params=pltpu.CompilerParams(vmem_limit_bytes=60 * MIB),
        cost_estimate=pl.CostEstimate(
            flops=3 * SLOTS * DEVICES * rows * M * 2 * C,
            bytes_accessed=4 * (SLOTS * M * 2 * C * 2 + arrived.size),
            transcendentals=0,
        ),
        name="legendre_analysis",
    )(waves, arrived.reshape((DEVICES, SLOTS) + tail), table, *((partial,) if last else ()))


def exchange(value, rows):
    pieces = value.reshape(DEVICES, SLOTS * rows, QB, LANES)
    moved = lax.all_to_all(pieces, AXES, split_axis=0, concat_axis=0, tiled=True)
    return moved.reshape(M * rows * QB, LANES)


def body(spectrum, legendre, wave_table, quad_weight, norm_gain, weight_in, bias_in, weight_out):
    weights = quad_weight[:, None]
    gain, bias = norm_gain[None, :], bias_in[None, :]
    tables = fourier_tables(wave_table)
    turned = [turn(chunk, wave_table, weights, legendre) for chunk in CHUNKS]
    arrived = [
        exchange(synth(chunk, wave_table, spectrum, legendre), len(chunk)) for chunk in CHUNKS
    ]
    back = [
        exchange(
            physics(len(chunk), value, tables, gain, weight_in, bias, weight_out), len(chunk)
        )
        for chunk, value in zip(CHUNKS, arrived)
    ]
    total = None
    for chunk, value, table in zip(CHUNKS, back, turned):
        total = analyse(chunk, wave_table, value, table, total)
    return total


def solution(mesh):
    return jax.shard_map(
        body,
        mesh=mesh,
        in_specs=(P(AXES, None, None), P(AXES, None, None), P(), P(), P(), P(), P(), P()),
        out_specs=P(AXES, None, None),
        check_vma=False,
    )
```
